32 devices in a mesh: dp: 4 (over y, x), row: 2 (over core), col: 4 (over z).
Axes of the slice: x: 2, y: 2, z: 4, core: 2. Of those that a mesh axis runs over, the one named last changes fastest.
Arguments:
- gradients: bfloat16 [4, 8192, 14336], P('dp', 'row', 'col'), may hold values from -6 to 6
- test_matrix: int32 [14336, 512], P('col'), may hold values from -3 to 3
- old_basis: float32 [8192, 512], P('row'), may hold values from -0.0625 to 0.0625
- first_moment: float32 [512, 14336], P(('dp', 'row'), 'col'), may hold values from -24 to 24
- second_moment: float32 [512, 14336], P(('dp', 'row'), 'col'), may hold values from 1 to 16
Outputs:
- projected: float32 [512, 14336], P(('dp', 'row'), 'col')
- first_moment_new: float32 [512, 14336], P(('dp', 'row'), 'col')
- second_moment_new: float32 [512, 14336], P(('dp', 'row'), 'col')
The draws below stay inside these ranges and needn't reach their ends.
All inputs are finite; a program needn't handle non-finite values.
Results may differ from the reference program's by a relative error of at most 0.0023.
Values sent between devices are 32-bit elements; how exact they have to be, the bound alone decides.
No kernel may reach another device: no remote copies, remote signals or barrier semaphores. Data moves between devices by JAX's collectives and lax.ppermute only.
A program may use at most 128 MiB of HBM per device.

```python
import math
import jax
import jax.numpy as jnp
from jax import lax

M = 8192
N = 14336
R = 512
REPLICAS = 4


def with_ends(drawn, key, least, high):
    longest = drawn.shape.index(max(drawn.shape))
    spots = []
    for shift in (0, 1):
        where = [jax.random.randint(jax.random.fold_in(key, axis), (), 0, length) for axis, length in enumerate(drawn.shape)]
        where[longest] = (where[longest] + shift) % drawn.shape[longest]
        spots.append(tuple(where))
    return drawn.at[spots[0]].set(least).at[spots[1]].set(high)


def steps_of(rng, shape, shards, low, high):
    level = 1.0
    for dim, blocks in shards:
        steps = jax.random.uniform(jax.random.fold_in(jax.random.fold_in(rng, 6), dim), (blocks,), jnp.float32, low / len(shards), high / len(shards))
        level = level * jnp.repeat(jnp.exp(steps), shape[dim] // blocks).reshape((-1,) + (1,) * (len(shape) - 1 - dim))
    return level


def bell_draw(stream_key, dims, spread, limit, split=(), dtype=jnp.bfloat16):
    array = jax.random.normal(stream_key, dims, jnp.float32) * spread
    if len(split) > 0:
        array = steps_of(stream_key, dims, split, -0.22, 0.18) * array
    return jnp.clip(array, min=-limit, max=limit).astype(dtype)


def setup_inputs(seed: int = 0) -> dict:
    arg_keys = jax.random.split(jax.random.key(seed), 6)
    return {
        "gradients": bell_draw(arg_keys[0], (REPLICAS, M, N), 1.0, 6.0, ((0, 4), (1, 2), (2, 4))),
        "test_matrix": with_ends(jax.random.randint(arg_keys[1], (N, R), -3, 4), jax.random.fold_in(arg_keys[1], 1), -3, 3).astype(jnp.int32),
        "old_basis": bell_draw(arg_keys[2], (M, R), M ** -0.5, 0.0625, ((0, 2),), jnp.float32),
        "first_moment": bell_draw(arg_keys[3], (R, N), 4.0, 24.0, ((0, 8), (1, 4)), jnp.float32),
        "second_moment": jnp.clip(jnp.exp(math.log(16.0) - 2.7725887 * jax.random.uniform(arg_keys[4], (R, N), jnp.float32) ** steps_of(arg_keys[4], (R, N), ((0, 8), (1, 4)), -0.2, 0.2)), 1.0, 16.0),
    }


highest = lax.Precision.HIGHEST

def reference(gradients, test_matrix, old_basis, first_moment, second_moment):
    test_values = test_matrix.astype(jnp.bfloat16)
    sketch = jnp.zeros((M, R), jnp.float32)
    for replica in range(REPLICAS):
        sketch = sketch + jnp.dot(gradients[replica].astype(jnp.float32), test_values.astype(jnp.float32), preferred_element_type=jnp.float32)
    gram_total = jnp.dot(sketch.T.astype(jnp.float32), sketch.astype(jnp.float32), precision=highest, preferred_element_type=jnp.float32)
    lower_factor = jnp.linalg.cholesky(gram_total)
    new_basis = jax.scipy.linalg.solve_triangular(lower_factor, sketch.T, lower=True).T
    basis_low = new_basis.astype(jnp.bfloat16)
    projected = jnp.zeros((R, N), jnp.float32)
    for replica in range(REPLICAS):
        projected = projected + jnp.dot(basis_low.T.astype(jnp.float32), gradients[replica].astype(jnp.float32), preferred_element_type=jnp.float32)
    correlation = jnp.dot(new_basis.T.astype(jnp.float32), old_basis.astype(jnp.float32), precision=highest, preferred_element_type=jnp.float32)
    turned_first = jnp.dot(correlation.astype(jnp.float32), first_moment.astype(jnp.float32), precision=highest, preferred_element_type=jnp.float32)
    turned_second = jnp.dot((correlation * correlation).astype(jnp.float32), second_moment.astype(jnp.float32), precision=highest, preferred_element_type=jnp.float32)
    first_new = 0.9 * turned_first + 0.1 * projected
    second_new = 0.95 * turned_second + 0.05 * projected * projected
    return (projected, first_new, second_new)
```

```python
import jax
import jax.numpy as jnp
from jax import lax
from jax.experimental import pallas as pl
from jax.experimental.pallas import tpu as pltpu
from jax.sharding import PartitionSpec as P

highest = lax.Precision.HIGHEST
BLOCK = 128


def contract(a, b, a_dim, b_dim):
    return lax.dot_general(
        a, b, (((a_dim,), (b_dim,)), ((), ())), precision=highest, preferred_element_type=jnp.float32
    )


def eliminate(block, inverse_ref):
    groups = BLOCK // 8
    left = [block[8 * g : 8 * g + 8] for g in range(groups)]
    row_ids = lax.broadcasted_iota(jnp.int32, (8, BLOCK), 0)
    lane_ids = lax.broadcasted_iota(jnp.int32, (8, BLOCK), 1)
    right = [(lane_ids == row_ids + 8 * g).astype(jnp.float32) for g in range(groups)]
    for j in range(BLOCK):
        own, sub = divmod(j, 8)
        row = left[own][sub : sub + 1]
        inv_row = right[own][sub : sub + 1]
        pivot = row[:, j : j + 1]
        recip = 1.0 / pivot
        inverse_ref[j : j + 1, :] = inv_row * lax.rsqrt(pivot)
        row_scaled = row * recip
        inv_scaled = inv_row * recip
        for g in range(own, groups):
            column = left[g][:, j : j + 1]
            if g == own:
                if sub == 7:
                    continue
                column = jnp.where(row_ids[:, :1] > sub, column, 0.0)
            left[g] = left[g] - column * row_scaled
            right[g] = right[g] - column * inv_scaled


def cholesky_kernel(gram_ref, inverse_ref, work_ref, rest_ref, diag_ref):
    size = gram_ref.shape[0]
    work_ref[...] = gram_ref[...]
    rows = lax.broadcasted_iota(jnp.int32, (size, size), 0)
    cols = lax.broadcasted_iota(jnp.int32, (size, size), 1)
    rest_ref[...] = (rows == cols).astype(jnp.float32)

    def step(k, _):
        at = pl.ds(pl.multiple_of(k * BLOCK, BLOCK), BLOCK)
        eliminate(work_ref[at, at], diag_ref)
        diag = diag_ref[...]
        below = lax.broadcasted_iota(jnp.int32, (size, BLOCK), 0) >= (k + 1) * BLOCK
        panel = jnp.where(below, work_ref[:, at], 0.0)
        factor = contract(panel, diag, 1, 1)
        done = contract(diag, rest_ref[at, :], 1, 0)
        inverse_ref[at, :] = done
        work_ref[...] -= contract(factor, factor, 1, 1)
        rest_ref[...] -= contract(factor, done, 1, 0)
        return 0

    lax.fori_loop(0, size // BLOCK, step, 0)


def inverse_cholesky(gram):
    size = gram.shape[0]
    return pl.pallas_call(
        cholesky_kernel,
        out_shape=jax.ShapeDtypeStruct((size, size), jnp.float32),
        in_specs=[pl.BlockSpec(memory_space=pltpu.VMEM)],
        out_specs=pl.BlockSpec(memory_space=pltpu.VMEM),
        scratch_shapes=[
            pltpu.VMEM((size, size), jnp.float32),
            pltpu.VMEM((size, size), jnp.float32),
            pltpu.VMEM((BLOCK, BLOCK), jnp.float32),
        ],
        compiler_params=pltpu.CompilerParams(vmem_limit_bytes=32 << 20),
        cost_estimate=pl.CostEstimate(flops=30_000_000_000, bytes_accessed=2_000_000, transcendentals=0),
    )(gram)


def bits_of(axis):
    return lax.axis_size(axis).bit_length() - 1


def own_bit(axis, bit):
    return (lax.axis_index(axis) >> bit) & 1


def swap(value, axis, bit):
    return lax.ppermute(value, axis, [(i, i ^ 1 << bit) for i in range(lax.axis_size(axis))])


def shifted(value, axis, by):
    size = lax.axis_size(axis)
    return lax.ppermute(value, axis, [(i, (i + by) % size) for i in range(size)])


def halve(value, axis, bit, dim=0):
    half = value.shape[dim] // 2
    me = own_bit(axis, bit)
    sent = lax.dynamic_slice_in_dim(value, (1 - me) * half, half, dim)
    kept = lax.dynamic_slice_in_dim(value, me * half, half, dim)
    return kept + swap(sent, axis, bit)


def double(value, axis, bit):
    other = swap(value, axis, bit)
    first = own_bit(axis, bit) == 0
    return jnp.concatenate([jnp.where(first, value, other), jnp.where(first, other, value)], 0)


def scatter_direct(value, axis):
    size = lax.axis_size(axis)
    part = value.shape[0] // size
    me = lax.axis_index(axis)
    total = lax.dynamic_slice_in_dim(value, me * part, part, 0)
    for by in range(1, size):
        total = total + shifted(
            lax.dynamic_slice_in_dim(value, (me + by) % size * part, part, 0), axis, by
        )
    return total


def gather_direct(value, axis):
    size = lax.axis_size(axis)
    me = lax.axis_index(axis)
    blocks = [value] + [shifted(value, axis, by) for by in range(1, size)]
    ordered = []
    for place in range(size):
        chosen = blocks[0]
        for by in range(1, size):
            chosen = jnp.where((me - by) % size == place, blocks[by], chosen)
        ordered.append(chosen)
    return jnp.concatenate(ordered, 0)


def scatter_ring(value, axis):
    size = lax.axis_size(axis)
    part = value.shape[0] // size
    me = lax.axis_index(axis)

    def block(place):
        return lax.dynamic_slice_in_dim(value, place % size * part, part, 0)

    total = block(me + size - 1)
    for step in range(1, size):
        total = shifted(total, axis, 1) + block(me + 2 * size - 1 - step)
    return total


def gather_ring(value, axis):
    size = lax.axis_size(axis)
    me = lax.axis_index(axis)
    blocks = [value]
    for _ in range(1, size):
        blocks.append(shifted(blocks[-1], axis, 1))
    ordered = []
    for place in range(size):
        chosen = blocks[0]
        for by in range(1, size):
            chosen = jnp.where((me - by) % size == place, blocks[by], chosen)
        ordered.append(chosen)
    return jnp.concatenate(ordered, 0)


def scatter_bits(value, axis, order):
    for bit in order:
        value = halve(value, axis, bit)
    return value


def gather_bits(value, axis, order):
    for bit in reversed(order):
        value = double(value, axis, bit)
    return value


def row_sum(value):
    for bit in range(bits_of("row")):
        value = value + swap(value, "row", bit)
    return value


def all_to_all(value):
    tail = value.shape[1:]
    dp_bits, row_bits = bits_of("dp"), bits_of("row")
    bits = [("dp", b) for b in reversed(range(dp_bits))] + [("row", b) for b in reversed(range(row_bits))]
    value = value.reshape((2,) * len(bits) + tail)
    for place in reversed(range(len(bits))):
        axis, bit = bits[place]
        me = own_bit(axis, bit)
        sent = lax.dynamic_index_in_dim(value, 1 - me, place, keepdims=True)
        kept = lax.dynamic_index_in_dim(value, me, place, keepdims=True)
        got = swap(sent, axis, bit)
        value = jnp.concatenate([jnp.where(me == 0, kept, got), jnp.where(me == 0, got, kept)], place)
    return value.reshape((1 << len(bits),) + tail)


def local(gradients, test_matrix, old_basis, first_moment, second_moment):
    grad = gradients[0]
    rows, cols = grad.shape
    rank_dev = first_moment.shape[0]
    group = lax.axis_size("dp") * lax.axis_size("row")
    rank = rank_dev * group
    wide = cols // group

    moments = jnp.stack([first_moment, second_moment])
    moments = moments.reshape(2, rank_dev, group, wide).transpose(2, 0, 1, 3)
    moments = all_to_all(moments)
    moments = moments.transpose(1, 0, 2, 3).reshape(2, rank, wide)

    test_values = test_matrix.astype(jnp.bfloat16)
    up = list(range(bits_of("dp")))
    down = up[::-1]
    unit = rows // 16
    plan = [(3, up), (3, down), (2, None), (3, up), (3, down), (2, None)]
    start = 0
    pieces = []
    for units, order in plan:
        size = units * unit
        part = jnp.dot(grad[start : start + size], test_values, preferred_element_type=jnp.float32)
        if order is None:
            part = scatter_bits(scatter_ring(part, "col"), "dp", up)
            part = gather_ring(gather_bits(part, "dp", up), "col")
        else:
            part = scatter_direct(scatter_bits(part, "dp", order), "col")
            part = gather_bits(gather_direct(part, "col"), "dp", order)
        pieces.append((start, size, part))
        start += size

    gram = 0.0
    inner = 0.0
    for start, size, part in pieces:
        gram = gram + contract(part, part, 0, 0)
        inner = inner + contract(part, old_basis[start : start + size], 0, 0)
    gram = row_sum(gram)
    inner = row_sum(inner)
    inverse = inverse_cholesky(gram)
    basis_low = jnp.concatenate(
        [contract(part, inverse, 1, 1).astype(jnp.bfloat16) for _, _, part in pieces], 0
    )

    correlation = contract(inverse, inner, 1, 0)
    turned = jnp.stack(
        [contract(correlation, moments[0], 1, 0), contract(correlation * correlation, moments[1], 1, 0)]
    )
    turned = turned.reshape(2, group, rank_dev, wide).transpose(1, 0, 2, 3)
    turned = all_to_all(turned)
    turned = turned.transpose(1, 2, 0, 3).reshape(2, rank_dev, cols)

    chunks = 4
    chunk = cols // chunks
    summed = []
    dp_bits, row_bits = bits_of("dp"), bits_of("row")
    for c in range(chunks):
        value = lax.dot_general(
            basis_low,
            grad[:, c * chunk : (c + 1) * chunk],
            (((0,), (0,)), ((), ())),
            preferred_element_type=jnp.float32,
        )
        value = value.reshape((2,) * (dp_bits + row_bits) + (rank_dev, chunk))
        places = [("row", b, dp_bits + row_bits - 1 - b) for b in range(row_bits)]
        dp_places = [("dp", b, dp_bits - 1 - b) for b in range(dp_bits)]
        for axis, bit, place in places + (dp_places if c % 2 else dp_places[::-1]):
            value = halve(value, axis, bit, place)
        summed.append(value.reshape(rank_dev, chunk))
    projected = jnp.concatenate(summed, 1)
    first_new = 0.9 * turned[0] + 0.1 * projected
    second_new = 0.95 * turned[1] + 0.05 * projected * projected
    return (projected, first_new, second_new)


def solution(mesh):
    in_specs = (
        P("dp", "row", "col"),
        P("col", None),
        P("row", None),
        P(("dp", "row"), "col"),
        P(("dp", "row"), "col"),
    )
    out_specs = (P(("dp", "row"), "col"), P(("dp", "row"), "col"), P(("dp", "row"), "col"))
    return jax.shard_map(local, mesh=mesh, in_specs=in_specs, out_specs=out_specs, check_vma=False)
```

```python
import functools

import jax
import jax.numpy as jnp
from jax import lax
from jax.experimental import pallas as pl
from jax.experimental.pallas import tpu as pltpu
from jax.sharding import PartitionSpec as P

highest = lax.Precision.HIGHEST
BLOCK = 128


def contract(a, b, a_dim, b_dim):
    return lax.dot_general(
        a, b, (((a_dim,), (b_dim,)), ((), ())), precision=highest, preferred_element_type=jnp.float32
    )


def eliminate(block, inverse_ref):
    groups = BLOCK // 8
    left = [block[8 * g : 8 * g + 8] for g in range(groups)]
    row_ids = lax.broadcasted_iota(jnp.int32, (8, BLOCK), 0)
    lane_ids = lax.broadcasted_iota(jnp.int32, (8, BLOCK), 1)
    right = [(lane_ids == row_ids + 8 * g).astype(jnp.float32) for g in range(groups)]
    for own in range(groups):
        at = 8 * own
        spread = {
            g: [jnp.broadcast_to(left[g][:, at + k : at + k + 1], (8, BLOCK)) for k in range(8)]
            for g in range(own, groups)
        }
        scaled = []
        for i in range(8):
            pivot = spread[own][i][i : i + 1]
            recip = 1.0 / pivot
            row, inv_row = left[own][i : i + 1], right[own][i : i + 1]
            inverse_ref[at + i : at + i + 1, :] = inv_row * lax.rsqrt(pivot)
            row, inv_row = row * recip, inv_row * recip
            scaled.append((row, inv_row))
            if i == 7:
                continue
            ratio = {k: spread[own][k][i : i + 1] * recip for k in range(i + 1, 8)}
            below = jnp.where(row_ids > i, spread[own][i], 0.0)
            left[own] = left[own] - below * row
            right[own] = right[own] - below * inv_row
            for g in range(own, groups):
                column = below if g == own else spread[g][i]
                for k in range(i + 1, 8):
                    spread[g][k] = spread[g][k] - column * ratio[k]
        for g in range(own + 1, groups):
            for i, (row, inv_row) in enumerate(scaled):
                left[g] = left[g] - spread[g][i] * row
                right[g] = right[g] - spread[g][i] * inv_row


def cholesky_kernel(index, work_in, rest_in, inverse_in, work_ref, rest_ref, inverse_ref, diag_ref):
    size = work_ref.shape[0]
    at = slice(index * BLOCK, (index + 1) * BLOCK)
    if index == 0:
        rows = lax.broadcasted_iota(jnp.int32, (size, size), 0)
        cols = lax.broadcasted_iota(jnp.int32, (size, size), 1)
        rest = (rows == cols).astype(jnp.float32)
    else:
        rest = rest_in[...]
        inverse_ref[...] = inverse_in[...]
    eliminate(work_in[at, at], diag_ref)
    diag = diag_ref[...]
    done = contract(diag, rest[at], 1, 0)
    inverse_ref[at, :] = done
    if index < size // BLOCK - 1:
        below = slice((index + 1) * BLOCK, size)
        factor = contract(work_in[below, at], diag, 1, 1)
        work_ref[below, below] = work_in[below, below] - contract(factor, factor, 1, 1)
        rest_ref[below, :] = rest[below] - contract(factor, done, 1, 0)


def cholesky_step(index, work, rest, inverse):
    size = work.shape[0]
    whole = jax.ShapeDtypeStruct((size, size), jnp.float32)
    spec = pl.BlockSpec(memory_space=pltpu.VMEM)
    return pl.pallas_call(
        functools.partial(cholesky_kernel, index),
        out_shape=[whole] * 3,
        in_specs=[spec] * 3,
        out_specs=[spec] * 3,
        scratch_shapes=[pltpu.VMEM((BLOCK, BLOCK), jnp.float32)],
        compiler_params=pltpu.CompilerParams(vmem_limit_bytes=32 << 20),
        cost_estimate=pl.CostEstimate(flops=7_000_000_000, bytes_accessed=6_000_000, transcendentals=0),
    )(work, rest, inverse)


def join(*values):
    return lax.optimization_barrier(values)


def bits_of(axis):
    return lax.axis_size(axis).bit_length() - 1


def own_bit(axis, bit):
    return (lax.axis_index(axis) >> bit) & 1


def flipped(value, axis, mask):
    return lax.ppermute(value, axis, [(i, i ^ mask) for i in range(lax.axis_size(axis))])


def swap(value, axis, bit):
    return flipped(value, axis, 1 << bit)


def shifted(value, axis):
    size = lax.axis_size(axis)
    return lax.ppermute(value, axis, [(i, (i + 1) % size) for i in range(size)])


def split_half(value, axis, bit, dim=0):
    half = value.shape[dim] // 2
    me = own_bit(axis, bit)
    sent = lax.dynamic_slice_in_dim(value, (1 - me) * half, half, dim)
    kept = lax.dynamic_slice_in_dim(value, me * half, half, dim)
    return sent, kept


def in_order(value, other, axis, bit):
    first = own_bit(axis, bit) == 0
    return jnp.concatenate([jnp.where(first, value, other), jnp.where(first, other, value)], 0)


def scatter_sends(value, axis):
    me = lax.axis_index(axis)
    kept = lax.dynamic_index_in_dim(value, me, 0, keepdims=False)
    return kept, [
        lax.dynamic_index_in_dim(value, me ^ mask, 0, keepdims=False)
        for mask in range(1, lax.axis_size(axis))
    ]


def flip_all(sends, axis):
    return [flipped(send, axis, mask) for mask, send in enumerate(sends, 1)]


def copies_to_all(value, axis):
    return flip_all([value] * (lax.axis_size(axis) - 1), axis)


def placed(value, others, axis):
    me = lax.axis_index(axis)
    blocks = [value] + list(others)
    return jnp.stack(
        [lax.select_n(me, *[blocks[p ^ i] for i in range(len(blocks))]) for p in range(len(blocks))]
    )


def ring_placed(blocks, axis):
    me = lax.axis_index(axis)
    size = len(blocks)
    return jnp.concatenate(
        [lax.select_n(me, *[blocks[(i - p) % size] for i in range(size)]) for p in range(size)], 0
    )


class Sum:
    def __init__(self, value):
        self.value = value
        self.steps = [("half", b) for b in range(bits_of("row"))]
        self.steps += [("scatter", "dp"), ("scatter", "col"), ("gather", "col"), ("gather", "dp")]
        self.steps += [("double", b) for b in reversed(range(bits_of("row")))]

    def start(self):
        kind, what = self.steps[0]
        if kind == "half":
            sent, self.kept = split_half(self.value, "row", what)
            self.got = [swap(sent, "row", what)]
        elif kind == "double":
            self.got = [swap(self.value, "row", what)]
        elif kind == "scatter":
            size = lax.axis_size(what)
            self.kept, sends = scatter_sends(self.value.reshape((size, -1) + self.value.shape[1:]), what)
            self.got = flip_all(sends, what)
        else:
            self.got = copies_to_all(self.value, what)

    def finish(self):
        kind, what = self.steps.pop(0)
        if kind in ("half", "scatter"):
            self.value = self.kept + sum(self.got)
        elif kind == "double":
            self.value = in_order(self.value, self.got[0], "row", what)
        else:
            self.value = placed(self.value, self.got, what).reshape((-1,) + self.value.shape[1:])


class Exchange:
    def __init__(self, value):
        self.tail = value.shape[1:]
        bits = [("dp", b) for b in reversed(range(bits_of("dp")))]
        self.bits = bits + [("row", b) for b in reversed(range(bits_of("row")))]
        self.value = value.reshape((2,) * len(self.bits) + self.tail)
        self.left = list(range(len(self.bits)))

    def start(self):
        place = self.left[-1]
        axis, bit = self.bits[place]
        me = own_bit(axis, bit)
        sent = lax.dynamic_index_in_dim(self.value, 1 - me, place, keepdims=True)
        self.kept = lax.dynamic_index_in_dim(self.value, me, place, keepdims=True)
        self.got = swap(sent, axis, bit)

    def finish(self):
        place = self.left.pop()
        me = own_bit(*self.bits[place])
        kept, got = self.kept, self.got
        self.value = jnp.concatenate([jnp.where(me == 0, kept, got), jnp.where(me == 0, got, kept)], place)

    def result(self):
        return self.value.reshape((1 << len(self.bits),) + self.tail)


def local(gradients, test_matrix, old_basis, first_moment, second_moment):
    grad = gradients[0]
    rows, cols = grad.shape
    rank_dev = first_moment.shape[0]
    dp_size, row_size, col_size = (lax.axis_size(a) for a in ("dp", "row", "col"))
    group = dp_size * row_size
    rank = rank_dev * group
    wide = cols // group
    dp_bits, row_bits = bits_of("dp"), bits_of("row")

    moments = jnp.stack([first_moment, second_moment])
    moments = moments.reshape(2, rank_dev, group, wide).transpose(2, 0, 1, 3)
    turn_in = Exchange(moments)

    test_values = test_matrix.astype(jnp.bfloat16)
    unit = rows // 32
    size_c, size_a, size_b = 10 * unit, 11 * unit, 11 * unit
    range_c, range_a, range_b = (0, size_c), (size_c, size_a), (size_c + size_a, size_b)

    def sketch(span):
        return jnp.dot(
            grad[span[0] : span[0] + span[1]], test_values, preferred_element_type=jnp.float32
        )

    low, high = 0, dp_bits - 1
    me_col = lax.axis_index("col")
    part_c = sketch(range_c)

    def block_c(back):
        return lax.dynamic_slice_in_dim(
            part_c, (me_col + 2 * col_size - back) % col_size * (size_c // col_size), size_c // col_size, 0
        )

    ring = shifted(block_c(1), "col")
    part_a, kept_a = split_half(sketch(range_a), "dp", low)
    got_a = swap(part_a, "dp", low)
    part_b, kept_b = split_half(sketch(range_b), "dp", high)
    got_b = swap(part_b, "dp", high)
    turn_in.start()
    ring, turn_in.got = join(ring, turn_in.got)
    turn_in.finish()
    ring = shifted(ring + block_c(2), "col")
    ring, got_a, got_b = join(ring, got_a, got_b)
    part_a, kept_a = split_half(kept_a + got_a, "dp", high)
    part_b, kept_b = split_half(kept_b + got_b, "dp", low)
    ring = shifted(ring + block_c(3), "col")
    got_a = swap(part_a, "dp", high)
    got_b = swap(part_b, "dp", low)
    ring, got_a, got_b = join(ring, got_a, got_b)
    part_ab = jnp.concatenate(
        [(kept_a + got_a).reshape(col_size, -1, rank), (kept_b + got_b).reshape(col_size, -1, rank)], 1
    )
    rows_ab = part_ab.shape[1]
    part_c = (ring + block_c(4)).reshape(dp_size, -1, rank)
    kept_ab, sends_ab = scatter_sends(part_ab, "col")
    kept_c, sends_c = scatter_sends(part_c, "dp")
    got_ab = flip_all(sends_ab, "col")
    got_c = flip_all(sends_c, "dp")
    turn_in.start()
    got_ab, got_c, turn_in.got = join(got_ab, got_c, turn_in.got)
    turn_in.finish()
    own_ab = kept_ab + sum(got_ab)
    own_c = kept_c + sum(got_c)

    own = jnp.concatenate([own_ab, own_c], 0)
    gram = Sum(contract(own, own, 0, 0))
    half = rows_ab // 2
    me_dp = lax.axis_index("dp")
    low_bit, high_bit = me_dp & 1, me_dp >> high & 1
    start_a = range_a[0] + low_bit * (size_a // 2) + high_bit * (size_a // 4) + me_col * half
    start_b = range_b[0] + high_bit * (size_b // 2) + low_bit * (size_b // 4) + me_col * half
    start_c = me_col * (size_c // col_size) + me_dp * (size_c // col_size // dp_size)
    own_old = jnp.concatenate(
        [
            lax.dynamic_slice_in_dim(old_basis, start_a, half, 0),
            lax.dynamic_slice_in_dim(old_basis, start_b, half, 0),
            lax.dynamic_slice_in_dim(old_basis, start_c, own_c.shape[0], 0),
        ],
        0,
    )
    inner = Sum(contract(own, own_old, 0, 0))

    for _ in range(row_bits):
        gram.start()
        (gram.got,) = join(gram.got)
        gram.finish()
    gram.start()
    got_ab = copies_to_all(own_ab, "col")
    got_c = copies_to_all(own_c, "dp")
    (gram.got,) = join(gram.got)
    gram.finish()
    gram.start()
    (gram.got,) = join(gram.got)
    gram.finish()
    gram.start()
    gram.got, got_ab, got_c, inner.value = join(gram.got, got_ab, got_c, inner.value)
    gram.finish()
    whole_ab = placed(own_ab, got_ab, "col")
    part_a = whole_ab[:, :half].reshape(-1, rank)
    part_b = whole_ab[:, half:].reshape(-1, rank)
    ring_c = [placed(own_c, got_c, "dp").reshape(-1, rank)]
    gram.start()
    got_a = swap(part_a, "dp", high)
    got_b = swap(part_b, "dp", low)
    ring_c.append(shifted(ring_c[0], "col"))
    (gram.got,) = join(gram.got)
    gram.finish()
    for _ in range(row_bits):
        gram.start()
        inner.start()
        gram.got, inner.got = join(gram.got, inner.got)
        gram.finish()
        inner.finish()
    work = gram.value
    rest = jnp.zeros_like(work)
    inverse = rest
    inner.start()
    work, rest, inverse = cholesky_step(0, work, rest, inverse)
    work, inner.got, got_a, got_b, ring_c[1] = join(work, inner.got, got_a, got_b, ring_c[1])
    inner.finish()
    part_a = in_order(part_a, got_a, "dp", high)
    part_b = in_order(part_b, got_b, "dp", low)
    got_a = swap(part_a, "dp", low)
    got_b = swap(part_b, "dp", high)
    ring_c.append(shifted(ring_c[1], "col"))
    inner.start()
    work, rest, inverse = cholesky_step(1, work, rest, inverse)
    work, inner.got, ring_c[2] = join(work, inner.got, ring_c[2])
    inner.finish()
    ring_c.append(shifted(ring_c[2], "col"))
    inner.start()
    work, rest, inverse = cholesky_step(2, work, rest, inverse)
    work, inner.got = join(work, inner.got)
    inner.finish()
    inner.start()
    work, rest, inverse = cholesky_step(3, work, rest, inverse)
    inverse, inner.got, got_a, got_b, ring_c[3] = join(inverse, inner.got, got_a, got_b, ring_c[3])
    inner.finish()

    def basis(part):
        return contract(part, inverse, 1, 1).astype(jnp.bfloat16)

    basis_low = jnp.concatenate(
        [
            ring_placed([basis(part) for part in ring_c], "col"),
            in_order(basis(part_a), basis(got_a), "dp", low),
            in_order(basis(part_b), basis(got_b), "dp", high),
        ],
        0,
    )

    chunks = 4
    chunk = cols // chunks

    def project(c):
        value = lax.dot_general(
            basis_low,
            grad[:, c * chunk : (c + 1) * chunk],
            (((0,), (0,)), ((), ())),
            preferred_element_type=jnp.float32,
        )
        return value.reshape((dp_size,) + (2,) * row_bits + (rank_dev, chunk))

    while len(turn_in.left) > 0:
        turn_in.start()
        inner_steps = len(inner.steps) > 0
        if inner_steps:
            inner.start()
            turn_in.got, inner.got = join(turn_in.got, inner.got)
            inner.finish()
        else:
            (turn_in.got,) = join(turn_in.got)
        turn_in.finish()
    while len(inner.steps) > 0:
        inner.start()
        (inner.got,) = join(inner.got)
        inner.finish()
    correlation = contract(inverse, inner.value, 1, 0)
    moments = turn_in.result().transpose(1, 0, 2, 3).reshape(2, rank, wide)
    turned = jnp.stack(
        [contract(correlation, moments[0], 1, 0), contract(correlation * correlation, moments[1], 1, 0)]
    )
    turn_out = Exchange(turned.reshape(2, group, rank_dev, wide).transpose(1, 0, 2, 3))

    values = [None] * chunks
    gots = [None] * chunks
    kepts = [None] * chunks
    values[0] = project(0)
    for r in range(chunks + 2):
        waits = []
        if 0 <= r - 1 < chunks:
            c = r - 1
            kepts[c], sends = scatter_sends(values[c], "dp")
            gots[c] = flip_all(sends, "dp")
        if r < chunks:
            value = values[r]
            for bit in range(row_bits):
                sent, kept = split_half(value, "row", bit, row_bits - bit)
                value = kept + swap(sent, "row", bit)
            values[r] = value
        if r + 1 < chunks:
            values[r + 1] = project(r + 1)
        if len(turn_out.left) > 0:
            turn_out.start()
        flat = (values, gots, turn_out.got)
        values, gots, turn_out.got = join(*flat)
        if len(turn_out.left) > 0:
            turn_out.finish()
        if 0 <= r - 1 < chunks:
            values[r - 1] = kepts[r - 1] + sum(gots[r - 1])
            gots[r - 1] = None
    while len(turn_out.left) > 0:
        turn_out.start()
        turn_out.finish()
    projected = jnp.concatenate([value.reshape(rank_dev, chunk) for value in values], 1)
    turned = turn_out.result().transpose(1, 2, 0, 3).reshape(2, rank_dev, cols)
    first_new = 0.9 * turned[0] + 0.1 * projected
    second_new = 0.95 * turned[1] + 0.05 * projected * projected
    return (projected, first_new, second_new)


def solution(mesh):
    in_specs = (
        P("dp", "row", "col"),
        P("col", None),
        P("row", None),
        P(("dp", "row"), "col"),
        P(("dp", "row"), "col"),
    )
    out_specs = (P(("dp", "row"), "col"), P(("dp", "row"), "col"), P(("dp", "row"), "col"))
    return jax.shard_map(local, mesh=mesh, in_specs=in_specs, out_specs=out_specs, check_vma=False)
```

```python
import functools

import jax
import jax.numpy as jnp
from jax import lax
from jax.experimental import pallas as pl
from jax.experimental.pallas import tpu as pltpu
from jax.sharding import PartitionSpec as P

highest = lax.Precision.HIGHEST
near = lax.Precision.HIGH
BLOCK = 128


def contract(a, b, a_dim, b_dim, precision=highest):
    return lax.dot_general(
        a, b, (((a_dim,), (b_dim,)), ((), ())), precision=precision, preferred_element_type=jnp.float32
    )


def eliminate(block, inverse_ref):
    groups = BLOCK // 8
    left = [block[8 * g : 8 * g + 8] for g in range(groups)]
    row_ids = lax.broadcasted_iota(jnp.int32, (8, BLOCK), 0)
    lane_ids = lax.broadcasted_iota(jnp.int32, (8, BLOCK), 1)
    right = [(lane_ids == row_ids + 8 * g).astype(jnp.float32) for g in range(groups)]
    for own in range(groups):
        at = 8 * own
        spread = {
            g: [jnp.broadcast_to(left[g][:, at + k : at + k + 1], (8, BLOCK)) for k in range(8)]
            for g in range(own, groups)
        }
        scaled = []
        for i in range(8):
            pivot = spread[own][i][i : i + 1]
            recip = 1.0 / pivot
            row, inv_row = left[own][i : i + 1], right[own][i : i + 1]
            inverse_ref[at + i : at + i + 1, :] = inv_row * lax.rsqrt(pivot)
            row, inv_row = row * recip, inv_row * recip
            scaled.append((row, inv_row))
            if i == 7:
                continue
            ratio = {k: spread[own][k][i : i + 1] * recip for k in range(i + 1, 8)}
            below = jnp.where(row_ids > i, spread[own][i], 0.0)
            left[own] = left[own] - below * row
            right[own] = right[own] - below * inv_row
            for g in range(own, groups):
                column = below if g == own else spread[g][i]
                for k in range(i + 1, 8):
                    spread[g][k] = spread[g][k] - column * ratio[k]
        for g in range(own + 1, groups):
            for i, (row, inv_row) in enumerate(scaled):
                left[g] = left[g] - spread[g][i] * row
                right[g] = right[g] - spread[g][i] * inv_row


def cholesky_kernel(index, work_in, rest_in, inverse_in, work_ref, rest_ref, inverse_ref, diag_ref):
    size = work_ref.shape[0]
    at = slice(index * BLOCK, (index + 1) * BLOCK)
    if index == 0:
        rows = lax.broadcasted_iota(jnp.int32, (size, size), 0)
        cols = lax.broadcasted_iota(jnp.int32, (size, size), 1)
        rest = (rows == cols).astype(jnp.float32)
    else:
        rest = rest_in[...]
        inverse_ref[...] = inverse_in[...]
    eliminate(work_in[at, at], diag_ref)
    diag = diag_ref[...]
    done = contract(diag, rest[at], 1, 0)
    inverse_ref[at, :] = done
    if index < size // BLOCK - 1:
        below = slice((index + 1) * BLOCK, size)
        factor = contract(work_in[below, at], diag, 1, 1)
        work_ref[below, below] = work_in[below, below] - contract(factor, factor, 1, 1)
        rest_ref[below, :] = rest[below] - contract(factor, done, 1, 0)


def cholesky_step(index, work, rest, inverse):
    size = work.shape[0]
    whole = jax.ShapeDtypeStruct((size, size), jnp.float32)
    spec = pl.BlockSpec(memory_space=pltpu.VMEM)
    return pl.pallas_call(
        functools.partial(cholesky_kernel, index),
        out_shape=[whole] * 3,
        in_specs=[spec] * 3,
        out_specs=[spec] * 3,
        scratch_shapes=[pltpu.VMEM((BLOCK, BLOCK), jnp.float32)],
        compiler_params=pltpu.CompilerParams(vmem_limit_bytes=32 << 20),
        cost_estimate=pl.CostEstimate(flops=1_000_000, bytes_accessed=100_000, transcendentals=0),
    )(work, rest, inverse)


def projection_kernel(sizes, first, tile, starts_ref, basis_ref, grad_ref, out_ref, held_ref, sems):
    step = pl.program_id(0)
    steps = pl.num_programs(0)

    def copies(index, slot):
        at = 0
        made = []
        for k, size in enumerate(sizes):
            source = grad_ref.at[
                pl.ds(pl.multiple_of(starts_ref[k], 16), size),
                pl.ds(pl.multiple_of(first + index * tile, 128), tile),
            ]
            made.append(pltpu.make_async_copy(source, held_ref.at[slot, pl.ds(at, size)], sems.at[slot, k]))
            at += size
        return made

    @pl.when(step == 0)
    def _():
        for copy in copies(0, 0):
            copy.start()

    @pl.when(step + 1 < steps)
    def _():
        for copy in copies(step + 1, (step + 1) % 2):
            copy.start()

    slot = step % 2
    for copy in copies(step, slot):
        copy.wait()
    out_ref[...] = lax.dot_general(
        basis_ref[...], held_ref[slot], (((0,), (0,)), ((), ())), preferred_element_type=jnp.float32
    )


def projection(starts, basis, grad, sizes, first, width, tile):
    rows, rank = basis.shape
    return pl.pallas_call(
        functools.partial(projection_kernel, sizes, first, tile),
        grid=(width // tile,),
        out_shape=jax.ShapeDtypeStruct((rank, width), jnp.float32),
        in_specs=[
            pl.BlockSpec(memory_space=pltpu.SMEM),
            pl.BlockSpec((rows, rank), lambda i: (0, 0), pipeline_mode=pl.Buffered(1)),
            pl.BlockSpec(memory_space=pl.ANY),
        ],
        out_specs=pl.BlockSpec((rank, tile), lambda i: (0, i)),
        scratch_shapes=[pltpu.VMEM((2, rows, tile), jnp.bfloat16), pltpu.SemaphoreType.DMA((2, len(sizes)))],
        compiler_params=pltpu.CompilerParams(vmem_limit_bytes=40 << 20),
        cost_estimate=pl.CostEstimate(flops=1_000_000, bytes_accessed=100_000, transcendentals=0),
    )(starts, basis, grad)


class Order:
    def __init__(self):
        self.mark = jnp.zeros((8, 128), jnp.float32)

    def __call__(self, *values):
        self.mark, *values = lax.optimization_barrier((self.mark,) + values)
        return values


def bits_of(axis):
    return lax.axis_size(axis).bit_length() - 1


def own_bit(axis, bit):
    return (lax.axis_index(axis) >> bit) & 1


def flipped(value, axis, mask):
    return lax.ppermute(value, axis, [(i, i ^ mask) for i in range(lax.axis_size(axis))])


def swap(value, axis, bit):
    return flipped(value, axis, 1 << bit)


def shifted(value, axis):
    size = lax.axis_size(axis)
    return lax.ppermute(value, axis, [(i, (i + 1) % size) for i in range(size)])


def split_half(value, axis, bit, dim=0):
    half = value.shape[dim] // 2
    me = own_bit(axis, bit)
    sent = lax.dynamic_slice_in_dim(value, (1 - me) * half, half, dim)
    kept = lax.dynamic_slice_in_dim(value, me * half, half, dim)
    return sent, kept


def in_order(value, other, axis, bit):
    first = own_bit(axis, bit) == 0
    return jnp.concatenate([jnp.where(first, value, other), jnp.where(first, other, value)], 0)


def scatter_sends(value, axis):
    me = lax.axis_index(axis)
    kept = lax.dynamic_index_in_dim(value, me, 0, keepdims=False)
    return kept, [
        lax.dynamic_index_in_dim(value, me ^ mask, 0, keepdims=False)
        for mask in range(1, lax.axis_size(axis))
    ]


def flip_all(sends, axis):
    return [flipped(send, axis, mask) for mask, send in enumerate(sends, 1)]


def copies_to_all(value, axis):
    return flip_all([value] * (lax.axis_size(axis) - 1), axis)


def placed(value, others, axis):
    me = lax.axis_index(axis)
    blocks = [value] + list(others)
    return jnp.stack(
        [lax.select_n(me, *[blocks[p ^ i] for i in range(len(blocks))]) for p in range(len(blocks))]
    )


def ring_placed(blocks, axis):
    me = lax.axis_index(axis)
    size = len(blocks)
    return jnp.concatenate(
        [lax.select_n(me, *[blocks[(i - p) % size] for i in range(size)]) for p in range(size)], 0
    )


class Sum:
    def __init__(self, value):
        self.value = value
        row = [("half", b) for b in range(bits_of("row"))]
        self.steps = row + [("scatter", "dp"), ("all", "col"), ("gather", "dp")]
        self.steps += [("double", b) for _, b in reversed(row)]

    def start(self):
        kind, what = self.steps[0]
        if kind == "half":
            sent, self.kept = split_half(self.value, "row", what)
            self.got = swap(sent, "row", what)
        elif kind == "double":
            self.got = swap(self.value, "row", what)
        elif kind == "scatter":
            size = lax.axis_size(what)
            self.kept, sends = scatter_sends(self.value.reshape((size, -1) + self.value.shape[1:]), what)
            self.got = flip_all(sends, what)
        else:
            self.got = copies_to_all(self.value, what)

    def finish(self):
        kind, what = self.steps.pop(0)
        if kind == "half":
            self.value = self.kept + self.got
        elif kind == "scatter":
            self.value = self.kept + sum(self.got)
        elif kind == "all":
            self.value = placed(self.value, self.got, what).sum(0)
        elif kind == "double":
            self.value = in_order(self.value, self.got, "row", what)
        else:
            self.value = placed(self.value, self.got, what).reshape((-1,) + self.value.shape[1:])


class Exchange:
    def __init__(self, value, dp_order):
        self.tail = value.shape[1:]
        dp_bits, row_bits = bits_of("dp"), bits_of("row")
        self.bits = [("dp", b) for b in reversed(range(dp_bits))] + [("row", b) for b in reversed(range(row_bits))]
        self.value = value.reshape((2,) * len(self.bits) + self.tail)
        self.left = [("row", b) for b in range(row_bits)] + [("dp", b) for b in dp_order]

    def start(self):
        axis, bit = self.left[0]
        place = self.bits.index((axis, bit))
        me = own_bit(axis, bit)
        sent = lax.dynamic_index_in_dim(self.value, 1 - me, place, keepdims=True)
        self.kept = lax.dynamic_index_in_dim(self.value, me, place, keepdims=True)
        self.got = swap(sent, axis, bit)

    def finish(self):
        axis, bit = self.left.pop(0)
        place = self.bits.index((axis, bit))
        me = own_bit(axis, bit)
        kept, got = self.kept, self.got
        self.value = jnp.concatenate([jnp.where(me == 0, kept, got), jnp.where(me == 0, got, kept)], place)

    def start_row(self):
        while self.left[1][0] == "row":
            self.start()
            self.finish()
        self.start()

    def result(self):
        return self.value.reshape((1 << len(self.bits),) + self.tail)


def exchanges(value, rank_dev, low, high):
    half = rank_dev // 2
    return [Exchange(value[:, :half], [low, high]), Exchange(value[:, half:], [high, low])]


def local(gradients, test_matrix, old_basis, first_moment, second_moment):
    join = Order()
    grad = gradients[0]
    rows, cols = grad.shape
    rank_dev = first_moment.shape[0]
    dp_size, row_size, col_size = (lax.axis_size(a) for a in ("dp", "row", "col"))
    group = dp_size * row_size
    rank = rank_dev * group
    wide = 2 * cols // group
    dp_bits, row_bits = bits_of("dp"), bits_of("row")
    low, high = 0, dp_bits - 1
    me_col, me_dp = lax.axis_index("col"), lax.axis_index("dp")
    at_low, at_high = own_bit("dp", low), own_bit("dp", high)

    test_values = test_matrix.astype(jnp.bfloat16)
    unit = rows // 32
    size_c, size = 10 * unit, 11 * unit
    base_a, base_b = size_c, size_c + size
    quarter_c = size_c // col_size
    half = size // 2

    both = jnp.concatenate([first_moment, second_moment], 1).reshape(rank_dev, group, wide).transpose(1, 0, 2)
    turns = exchanges(both, rank_dev, low, high)
    for turn in turns:
        turn.start_row()
    whole = jnp.dot(grad, test_values, preferred_element_type=jnp.float32)
    whole, turns[0].got, turns[1].got = join(whole, turns[0].got, turns[1].got)

    def block_c(back):
        return lax.dynamic_slice_in_dim(whole, (me_col + 2 * col_size - back) % col_size * quarter_c, quarter_c, 0)

    got_a = swap(lax.dynamic_slice_in_dim(whole, base_a + (1 - at_low) * half, half, 0), "dp", low)
    got_b = swap(lax.dynamic_slice_in_dim(whole, base_b + (1 - at_high) * half, half, 0), "dp", high)
    ring = shifted(block_c(1), "col")
    (ring,) = join(ring)
    ring = shifted(ring + block_c(2), "col")
    for turn in turns:
        turn.finish()
    got_a, got_b = join(got_a, got_b)
    kept_a = lax.dynamic_slice_in_dim(whole, base_a + at_low * half, half, 0)
    kept_b = lax.dynamic_slice_in_dim(whole, base_b + at_high * half, half, 0)
    sent_a, kept_a = split_half(kept_a + got_a, "dp", high)
    sent_b, kept_b = split_half(kept_b + got_b, "dp", low)
    got_a = swap(sent_a, "dp", high)
    got_b = swap(sent_b, "dp", low)
    (ring,) = join(ring)
    ring = shifted(ring + block_c(3), "col")
    got_a, got_b = join(got_a, got_b)
    part_ab = jnp.concatenate(
        [(kept_a + got_a).reshape(col_size, -1, rank), (kept_b + got_b).reshape(col_size, -1, rank)], 1
    ).reshape(2, 2, -1, rank)
    sent_ab, kept_ab = split_half(part_ab, "col", 0, 1)
    got_ab = swap(sent_ab, "col", 0)
    for turn in turns:
        turn.start()
    (ring,) = join(ring)
    sent_c, kept_c = split_half(ring + block_c(4), "dp", low)
    got_c = swap(sent_c, "dp", low)
    got_ab, got_c, turns[0].got, turns[1].got = join(got_ab, got_c, turns[0].got, turns[1].got)
    sent_ab, kept_ab = split_half(kept_ab + got_ab, "col", 1, 0)
    got_ab = swap(sent_ab, "col", 1)
    sent_c, kept_c = split_half(kept_c + got_c, "dp", high)
    got_c = swap(sent_c, "dp", high)
    for turn in turns:
        turn.finish()
        turn.start()
    got_ab, got_c, turns[0].got, turns[1].got = join(got_ab, got_c, turns[0].got, turns[1].got)
    own_ab = (kept_ab + got_ab).reshape(-1, rank)
    own_c = kept_c + got_c

    got_ab = swap(own_ab, "col", 1)
    got_c = swap(own_c, "dp", high)
    own = jnp.concatenate([own_ab, own_c], 0)
    gram = Sum(contract(own, own, 0, 0))
    for _ in range(row_bits - 1):
        gram.start()
        (gram.got,) = join(gram.got)
        gram.finish()
    gram.start()
    gram.got, got_c = join(gram.got, got_c)
    gram.finish()
    own_c = in_order(own_c, got_c, "dp", high)
    gram.start()
    got_c = swap(own_c, "dp", low)
    gram.got, got_c, got_ab = join(gram.got, got_c, got_ab)
    gram.finish()
    gram.start()
    own_ab = in_order(own_ab, got_ab, "col", 1)
    got_ab = swap(own_ab, "col", 0)
    (gram.got,) = join(gram.got)
    gram.finish()
    gram.start()
    ring_c = [in_order(own_c, got_c, "dp", low)]
    ring_c.append(shifted(ring_c[0], "col"))
    (gram.got,) = join(gram.got)
    gram.finish()
    for _ in range(row_bits):
        gram.start()
        (gram.got,) = join(gram.got)
        gram.finish()
    (got_ab,) = join(got_ab)

    def part_of(which):
        first = own_bit("col", 0) == 0
        mine, other = (block.reshape(2, 2, -1, rank)[:, which] for block in (own_ab, got_ab))
        pair = jnp.stack([jnp.where(first, mine, other), jnp.where(first, other, mine)], 1)
        return pair.reshape(-1, rank)

    part_a, part_b = part_of(0), part_of(1)
    got_a = swap(part_a, "dp", high)
    got_b = swap(part_b, "dp", low)
    for turn in turns:
        turn.finish()
    work = gram.value
    rest = jnp.zeros_like(work)
    inverse = rest
    work, rest, inverse = cholesky_step(0, work, rest, inverse)
    work, rest, inverse = cholesky_step(1, work, rest, inverse)
    work, got_a, got_b, ring_c[1] = join(work, got_a, got_b, ring_c[1])
    part_a = in_order(part_a, got_a, "dp", high)
    part_b = in_order(part_b, got_b, "dp", low)
    got_a = swap(part_a, "dp", low)
    got_b = swap(part_b, "dp", high)
    ring_c.append(shifted(ring_c[1], "col"))
    work, rest, inverse = cholesky_step(2, work, rest, inverse)
    work, rest, inverse = cholesky_step(3, work, rest, inverse)
    inverse, ring_c[2] = join(inverse, ring_c[2])
    ring_c.append(shifted(ring_c[2], "col"))

    def old_rows(base, bit):
        return lax.dynamic_slice_in_dim(old_basis, base + bit * half, half, 0)

    def old_ring(back):
        return lax.dynamic_slice_in_dim(old_basis, (me_col + col_size - back) % col_size * quarter_c, quarter_c, 0)

    def basis(part):
        return contract(part, inverse, 1, 1, near).astype(jnp.bfloat16)

    basis_a, basis_b = basis(part_a), basis(part_b)
    basis_c = [basis(ring_c[0]), basis(ring_c[1]), basis(ring_c[2])]
    inner = contract(part_a, old_rows(base_a, at_low), 0, 0, near)
    inner = inner + contract(part_b, old_rows(base_b, at_high), 0, 0, near)
    for back in range(3):
        inner = inner + contract(ring_c[back], old_ring(back), 0, 0, near)
    got_a, got_b, ring_c[3], inner, basis_a, basis_b, basis_c = join(
        got_a, got_b, ring_c[3], inner, basis_a, basis_b, basis_c
    )
    inner = inner + contract(got_a, old_rows(base_a, 1 - at_low), 0, 0, near)
    inner = inner + contract(got_b, old_rows(base_b, 1 - at_high), 0, 0, near)
    inner = inner + contract(ring_c[3], old_ring(3), 0, 0, near)
    inner_got = swap(inner, "row", 0)
    basis_low = jnp.concatenate(basis_c + [basis(ring_c[3]), basis_a, basis(got_a), basis_b, basis(got_b)], 0)
    starts = [(me_col + col_size - back) % col_size * quarter_c for back in range(col_size)]
    starts += [base_a + at_low * half, base_a + (1 - at_low) * half]
    starts += [base_b + at_high * half, base_b + (1 - at_high) * half]
    starts = jnp.stack(starts).astype(jnp.int32)
    sizes = [quarter_c] * col_size + [half] * 4
    basis_low, inner_got = join(basis_low, inner_got)
    inner = inner + inner_got
    for bit in range(1, row_bits):
        inner = inner + swap(inner, "row", bit)
    correlation = contract(inverse, inner, 1, 0)
    place = me_dp * row_size + lax.axis_index("row")
    turner = jnp.where(place < group // 2, correlation, correlation * correlation)
    turned = jnp.concatenate([turn.result() for turn in turns], 1).reshape(rank, wide)
    turned = contract(turner, turned, 1, 0)
    turns = exchanges(turned.reshape(group, rank_dev, wide), rank_dev, low, high)

    chunks = 4
    tile = cols // 7
    widths = [2 * tile, 2 * tile, 2 * tile, tile]
    values, kepts, gots = [None] * chunks, [None] * chunks, [None] * chunks

    def project(c):
        value = projection(starts, basis_low, grad, sizes, sum(widths[:c]), widths[c], tile)
        values[c] = value.reshape((2,) * (dp_bits + row_bits) + (rank_dev, widths[c]))

    def start(c, axis, bit):
        place = dp_bits - 1 - bit if axis == "dp" else dp_bits + row_bits - 1 - bit
        sent, kepts[c] = split_half(values[c], axis, bit, place)
        gots[c] = swap(sent, axis, bit)

    def finish(c):
        values[c] = kepts[c] + gots[c]

    def start_row(c):
        for bit in range(row_bits):
            if bit > 0:
                finish(c)
            start(c, "row", bit)

    for turn in turns:
        turn.start_row()
    project(0)
    basis_low, values[0], turns[0].got, turns[1].got = join(basis_low, values[0], turns[0].got, turns[1].got)
    for turn in turns:
        turn.finish()
        turn.start()
    start_row(0)
    project(1)
    basis_low, values[1], gots[0] = join(basis_low, values[1], gots[0])
    finish(0)
    start(0, "dp", low)
    start_row(1)
    project(2)
    basis_low, values[2], gots[1], turns[0].got, turns[1].got = join(
        basis_low, values[2], gots[1], turns[0].got, turns[1].got
    )
    finish(1)
    start(1, "dp", high)
    for turn in turns:
        turn.finish()
        turn.start()
    start_row(2)
    project(3)
    values[3], gots[2], gots[0] = join(values[3], gots[2], gots[0])
    finish(2)
    finish(0)
    start_row(3)
    start(2, "dp", low)
    gots[3], gots[1], turns[0].got, turns[1].got = join(gots[3], gots[1], turns[0].got, turns[1].got)
    finish(1)
    finish(3)
    start(0, "dp", high)
    start(1, "dp", low)
    start(3, "dp", high)
    for turn in turns:
        turn.finish()
    gots[0], gots[2] = join(gots[0], gots[2])
    finish(0)
    finish(2)
    start(2, "dp", high)
    gots[1], gots[3] = join(gots[1], gots[3])
    finish(1)
    finish(3)
    start(3, "dp", low)
    gots[2], gots[3] = join(gots[2], gots[3])
    finish(2)
    finish(3)
    projected = jnp.concatenate([value.reshape(rank_dev, width) for value, width in zip(values, widths, strict=True)], 1)
    turned = jnp.concatenate([turn.result() for turn in turns], 1).reshape(2, group // 2, rank_dev, wide).transpose(0, 2, 1, 3).reshape(2, rank_dev, cols)
    first_new = 0.9 * turned[0] + 0.1 * projected
    second_new = 0.95 * turned[1] + 0.05 * projected * projected
    return (projected, first_new, second_new)


def solution(mesh):
    in_specs = (
        P("dp", "row", "col"),
        P("col", None),
        P("row", None),
        P(("dp", "row"), "col"),
        P(("dp", "row"), "col"),
    )
    out_specs = (P(("dp", "row"), "col"), P(("dp", "row"), "col"), P(("dp", "row"), "col"))
    return jax.shard_map(local, mesh=mesh, in_specs=in_specs, out_specs=out_specs, check_vma=False)
```

```python
import functools

import jax
import jax.numpy as jnp
from jax import lax
from jax.experimental import pallas as pl
from jax.experimental.pallas import tpu as pltpu
from jax.sharding import PartitionSpec as P

highest = lax.Precision.HIGHEST
near = lax.Precision.HIGH
BLOCK = 128


def contract(a, b, a_dim, b_dim, precision=highest):
    return lax.dot_general(
        a, b, (((a_dim,), (b_dim,)), ((), ())), precision=precision, preferred_element_type=jnp.float32
    )


def eliminate(block, inverse_ref):
    groups = BLOCK // 8
    left = [block[8 * g : 8 * g + 8] for g in range(groups)]
    row_ids = lax.broadcasted_iota(jnp.int32, (8, BLOCK), 0)
    lane_ids = lax.broadcasted_iota(jnp.int32, (8, BLOCK), 1)
    right = [(lane_ids == row_ids + 8 * g).astype(jnp.float32) for g in range(groups)]
    for own in range(groups):
        at = 8 * own
        spread = {
            g: [jnp.broadcast_to(left[g][:, at + k : at + k + 1], (8, BLOCK)) for k in range(8)]
            for g in range(own, groups)
        }
        scaled = []
        for i in range(8):
            pivot = spread[own][i][i : i + 1]
            recip = 1.0 / pivot
            row, inv_row = left[own][i : i + 1], right[own][i : i + 1]
            inverse_ref[at + i : at + i + 1, :] = inv_row * lax.rsqrt(pivot)
            row, inv_row = row * recip, inv_row * recip
            scaled.append((row, inv_row))
            if i == 7:
                continue
            ratio = {k: spread[own][k][i : i + 1] * recip for k in range(i + 1, 8)}
            below = jnp.where(row_ids > i, spread[own][i], 0.0)
            left[own] = left[own] - below * row
            right[own] = right[own] - below * inv_row
            for g in range(own, groups):
                column = below if g == own else spread[g][i]
                for k in range(i + 1, 8):
                    spread[g][k] = spread[g][k] - column * ratio[k]
        for g in range(own + 1, groups):
            for i, (row, inv_row) in enumerate(scaled):
                left[g] = left[g] - spread[g][i] * row
                right[g] = right[g] - spread[g][i] * inv_row


def cholesky_kernel(index, work_in, rest_in, inverse_in, work_ref, rest_ref, inverse_ref, diag_ref):
    size = work_ref.shape[0]
    at = slice(index * BLOCK, (index + 1) * BLOCK)
    if index == 0:
        rows = lax.broadcasted_iota(jnp.int32, (size, size), 0)
        cols = lax.broadcasted_iota(jnp.int32, (size, size), 1)
        rest = (rows == cols).astype(jnp.float32)
    else:
        rest = rest_in[...]
        inverse_ref[...] = inverse_in[...]
    eliminate(work_in[at, at], diag_ref)
    diag = diag_ref[...]
    done = contract(diag, rest[at], 1, 0)
    inverse_ref[at, :] = done
    if index < size // BLOCK - 1:
        below = slice((index + 1) * BLOCK, size)
        factor = contract(work_in[below, at], diag, 1, 1)
        work_ref[below, below] = work_in[below, below] - contract(factor, factor, 1, 1)
        rest_ref[below, :] = rest[below] - contract(factor, done, 1, 0)


def cholesky_step(index, work, rest, inverse):
    size = work.shape[0]
    whole = jax.ShapeDtypeStruct((size, size), jnp.float32)
    spec = pl.BlockSpec(memory_space=pltpu.VMEM)
    return pl.pallas_call(
        functools.partial(cholesky_kernel, index),
        out_shape=[whole] * 3,
        in_specs=[spec] * 3,
        out_specs=[spec] * 3,
        scratch_shapes=[pltpu.VMEM((BLOCK, BLOCK), jnp.float32)],
        compiler_params=pltpu.CompilerParams(vmem_limit_bytes=32 << 20),
        cost_estimate=pl.CostEstimate(flops=1_000_000, bytes_accessed=100_000, transcendentals=0),
    )(work, rest, inverse)


def projection_kernel(sizes, first, tile, starts_ref, basis_ref, grad_ref, out_ref, held_ref, sems):
    step = pl.program_id(0)
    steps = pl.num_programs(0)

    def copies(index, slot):
        at = 0
        made = []
        for k, size in enumerate(sizes):
            source = grad_ref.at[
                pl.ds(pl.multiple_of(starts_ref[k], 16), size),
                pl.ds(pl.multiple_of(first + index * tile, 128), tile),
            ]
            made.append(pltpu.make_async_copy(source, held_ref.at[slot, pl.ds(at, size)], sems.at[slot, k]))
            at += size
        return made

    @pl.when(step == 0)
    def _():
        for copy in copies(0, 0):
            copy.start()

    @pl.when(step + 1 < steps)
    def _():
        for copy in copies(step + 1, (step + 1) % 2):
            copy.start()

    slot = step % 2
    for copy in copies(step, slot):
        copy.wait()
    out_ref[...] = lax.dot_general(
        basis_ref[...], held_ref[slot], (((0,), (0,)), ((), ())), preferred_element_type=jnp.float32
    )


def projection(starts, basis, grad, sizes, first, width, tile):
    rows, rank = basis.shape
    return pl.pallas_call(
        functools.partial(projection_kernel, sizes, first, tile),
        grid=(width // tile,),
        out_shape=jax.ShapeDtypeStruct((rank, width), jnp.float32),
        in_specs=[
            pl.BlockSpec(memory_space=pltpu.SMEM),
            pl.BlockSpec((rows, rank), lambda i: (0, 0), pipeline_mode=pl.Buffered(1)),
            pl.BlockSpec(memory_space=pl.ANY),
        ],
        out_specs=pl.BlockSpec((rank, tile), lambda i: (0, i)),
        scratch_shapes=[pltpu.VMEM((2, rows, tile), jnp.bfloat16), pltpu.SemaphoreType.DMA((2, len(sizes)))],
        compiler_params=pltpu.CompilerParams(vmem_limit_bytes=40 << 20),
        cost_estimate=pl.CostEstimate(flops=1_000_000, bytes_accessed=100_000, transcendentals=0),
    )(starts, basis, grad)


class Order:
    def __init__(self):
        self.mark = jnp.zeros((8, 128), jnp.float32)

    def __call__(self, *values):
        self.mark, *values = lax.optimization_barrier((self.mark,) + values)
        return values


def bits_of(axis):
    return lax.axis_size(axis).bit_length() - 1


def own_bit(axis, bit):
    return (lax.axis_index(axis) >> bit) & 1


def flipped(value, axis, mask):
    return lax.ppermute(value, axis, [(i, i ^ mask) for i in range(lax.axis_size(axis))])


def swap(value, axis, bit):
    return flipped(value, axis, 1 << bit)


def shifted(value, axis):
    size = lax.axis_size(axis)
    return lax.ppermute(value, axis, [(i, (i + 1) % size) for i in range(size)])


def split_half(value, axis, bit, dim=0):
    half = value.shape[dim] // 2
    me = own_bit(axis, bit)
    sent = lax.dynamic_slice_in_dim(value, (1 - me) * half, half, dim)
    kept = lax.dynamic_slice_in_dim(value, me * half, half, dim)
    return sent, kept


def in_order(value, other, axis, bit):
    first = own_bit(axis, bit) == 0
    return jnp.concatenate([jnp.where(first, value, other), jnp.where(first, other, value)], 0)


def scatter_sends(value, axis):
    me = lax.axis_index(axis)
    kept = lax.dynamic_index_in_dim(value, me, 0, keepdims=False)
    return kept, [
        lax.dynamic_index_in_dim(value, me ^ mask, 0, keepdims=False)
        for mask in range(1, lax.axis_size(axis))
    ]


def flip_all(sends, axis):
    return [flipped(send, axis, mask) for mask, send in enumerate(sends, 1)]


def copies_to_all(value, axis):
    return flip_all([value] * (lax.axis_size(axis) - 1), axis)


def placed(value, others, axis):
    me = lax.axis_index(axis)
    blocks = [value] + list(others)
    return jnp.stack(
        [lax.select_n(me, *[blocks[p ^ i] for i in range(len(blocks))]) for p in range(len(blocks))]
    )


def ring_placed(blocks, axis):
    me = lax.axis_index(axis)
    size = len(blocks)
    return jnp.concatenate(
        [lax.select_n(me, *[blocks[(i - p) % size] for i in range(size)]) for p in range(size)], 0
    )


class Sum:
    def __init__(self, value):
        self.value = value
        row = [("half", b) for b in range(bits_of("row"))]
        self.steps = row + [("scatter", "dp"), ("all", "col"), ("gather", "dp")]
        self.steps += [("double", b) for _, b in reversed(row)]

    def start(self):
        kind, what = self.steps[0]
        if kind == "half":
            sent, self.kept = split_half(self.value, "row", what)
            self.got = swap(sent, "row", what)
        elif kind == "double":
            self.got = swap(self.value, "row", what)
        elif kind == "scatter":
            size = lax.axis_size(what)
            self.kept, sends = scatter_sends(self.value.reshape((size, -1) + self.value.shape[1:]), what)
            self.got = flip_all(sends, what)
        else:
            self.got = copies_to_all(self.value, what)

    def finish(self):
        kind, what = self.steps.pop(0)
        if kind == "half":
            self.value = self.kept + self.got
        elif kind == "scatter":
            self.value = self.kept + sum(self.got)
        elif kind == "all":
            self.value = placed(self.value, self.got, what).sum(0)
        elif kind == "double":
            self.value = in_order(self.value, self.got, "row", what)
        else:
            self.value = placed(self.value, self.got, what).reshape((-1,) + self.value.shape[1:])


class Exchange:
    def __init__(self, value, dp_order, row=True):
        self.tail = value.shape[1:]
        dp_bits, row_bits = bits_of("dp"), bits_of("row")
        self.bits = [("dp", b) for b in reversed(range(dp_bits))] + [("row", b) for b in reversed(range(row_bits))]
        self.value = value.reshape((2,) * len(self.bits) + self.tail)
        self.left = [("row", b) for b in range(row_bits) if row] + [("dp", b) for b in dp_order]

    def start(self):
        axis, bit = self.left[0]
        place = self.bits.index((axis, bit))
        me = own_bit(axis, bit)
        sent = lax.dynamic_index_in_dim(self.value, 1 - me, place, keepdims=True)
        self.kept = lax.dynamic_index_in_dim(self.value, me, place, keepdims=True)
        self.got = swap(sent, axis, bit)

    def finish(self):
        axis, bit = self.left.pop(0)
        place = self.bits.index((axis, bit))
        me = own_bit(axis, bit)
        kept, got = self.kept, self.got
        self.value = jnp.concatenate([jnp.where(me == 0, kept, got), jnp.where(me == 0, got, kept)], place)

    def start_row(self):
        while len(self.left) > 1 and self.left[1][0] == "row":
            self.start()
            self.finish()
        self.start()

    def split(self, low, high):
        half = self.tail[0] // 2
        return [
            Exchange(self.result()[:, at : at + half], order, False)
            for at, order in ((0, [low, high]), (half, [high, low]))
        ]

    def result(self):
        return self.value.reshape((1 << len(self.bits),) + self.tail)


class Part:
    def __init__(self, value, dp_bits, row_bits):
        self.value = value
        self.bits = (dp_bits, row_bits)

    def start(self, axis, bit):
        dp_bits, row_bits = self.bits
        place = dp_bits - 1 - bit if axis == "dp" else dp_bits + row_bits - 1 - bit
        sent, self.kept = split_half(self.value, axis, bit, place)
        self.got = swap(sent, axis, bit)

    def finish(self):
        self.value = self.kept + self.got

    def start_row(self):
        for bit in range(self.bits[1]):
            if bit > 0:
                self.finish()
            self.start("row", bit)

    def halves(self):
        cut = self.value.shape[-1] // 2
        return [Part(self.value[..., :cut], *self.bits), Part(self.value[..., cut:], *self.bits)]


def local(gradients, test_matrix, old_basis, first_moment, second_moment):
    join = Order()
    grad = gradients[0]
    rows, cols = grad.shape
    rank_dev = first_moment.shape[0]
    dp_size, row_size, col_size = (lax.axis_size(a) for a in ("dp", "row", "col"))
    group = dp_size * row_size
    rank = rank_dev * group
    wide = 2 * cols // group
    dp_bits, row_bits = bits_of("dp"), bits_of("row")
    low, high = 0, dp_bits - 1
    me_col, me_dp = lax.axis_index("col"), lax.axis_index("dp")
    at_low, at_high = own_bit("dp", low), own_bit("dp", high)

    test_values = test_matrix.astype(jnp.bfloat16)
    unit = rows // 32
    size_c, size = 10 * unit, 11 * unit
    base_a, base_b = size_c, size_c + size
    quarter_c = size_c // col_size
    half = size // 2

    both = jnp.concatenate([first_moment, second_moment], 1).reshape(rank_dev, group, wide).transpose(1, 0, 2)
    turn = Exchange(both, [])
    turn.start_row()
    whole = jnp.dot(grad, test_values, preferred_element_type=jnp.float32)
    whole, turn.got = join(whole, turn.got)

    def block_c(back):
        return lax.dynamic_slice_in_dim(whole, (me_col + 2 * col_size - back) % col_size * quarter_c, quarter_c, 0)

    got_a = swap(lax.dynamic_slice_in_dim(whole, base_a + (1 - at_low) * half, half, 0), "dp", low)
    got_b = swap(lax.dynamic_slice_in_dim(whole, base_b + (1 - at_high) * half, half, 0), "dp", high)
    ring = shifted(block_c(1), "col")
    (ring,) = join(ring)
    ring = shifted(ring + block_c(2), "col")
    turn.finish()
    turns = turn.split(low, high)
    got_a, got_b = join(got_a, got_b)
    kept_a = lax.dynamic_slice_in_dim(whole, base_a + at_low * half, half, 0)
    kept_b = lax.dynamic_slice_in_dim(whole, base_b + at_high * half, half, 0)
    sent_a, kept_a = split_half(kept_a + got_a, "dp", high)
    sent_b, kept_b = split_half(kept_b + got_b, "dp", low)
    got_a = swap(sent_a, "dp", high)
    got_b = swap(sent_b, "dp", low)
    (ring,) = join(ring)
    ring = shifted(ring + block_c(3), "col")
    got_a, got_b = join(got_a, got_b)
    part_ab = jnp.concatenate(
        [(kept_a + got_a).reshape(col_size, -1, rank), (kept_b + got_b).reshape(col_size, -1, rank)], 1
    ).reshape(2, 2, -1, rank)
    sent_ab, kept_ab = split_half(part_ab, "col", 0, 1)
    got_ab = swap(sent_ab, "col", 0)
    for turn in turns:
        turn.start()
    (ring,) = join(ring)
    sent_c, kept_c = split_half(ring + block_c(4), "dp", low)
    got_c = swap(sent_c, "dp", low)
    got_ab, got_c, turns[0].got, turns[1].got = join(got_ab, got_c, turns[0].got, turns[1].got)
    sent_ab, kept_ab = split_half(kept_ab + got_ab, "col", 1, 0)
    got_ab = swap(sent_ab, "col", 1)
    sent_c, kept_c = split_half(kept_c + got_c, "dp", high)
    got_c = swap(sent_c, "dp", high)
    for turn in turns:
        turn.finish()
        turn.start()
    got_ab, got_c, turns[0].got, turns[1].got = join(got_ab, got_c, turns[0].got, turns[1].got)
    own_ab = (kept_ab + got_ab).reshape(-1, rank)
    own_c = kept_c + got_c

    got_ab = swap(own_ab, "col", 1)
    got_c = swap(own_c, "dp", high)
    own = jnp.concatenate([own_ab, own_c], 0)
    gram = Sum(contract(own, own, 0, 0))
    for _ in range(row_bits - 1):
        gram.start()
        (gram.got,) = join(gram.got)
        gram.finish()
    gram.start()
    gram.got, got_c = join(gram.got, got_c)
    gram.finish()
    own_c = in_order(own_c, got_c, "dp", high)
    gram.start()
    got_c = swap(own_c, "dp", low)
    gram.got, got_c, got_ab = join(gram.got, got_c, got_ab)
    gram.finish()
    gram.start()
    own_ab = in_order(own_ab, got_ab, "col", 1)
    got_ab = swap(own_ab, "col", 0)
    (gram.got,) = join(gram.got)
    gram.finish()
    gram.start()
    ring_c = [in_order(own_c, got_c, "dp", low)]
    ring_c.append(shifted(ring_c[0], "col"))
    (gram.got,) = join(gram.got)
    gram.finish()
    for _ in range(row_bits):
        gram.start()
        (gram.got,) = join(gram.got)
        gram.finish()
    (got_ab,) = join(got_ab)

    def part_of(which):
        first = own_bit("col", 0) == 0
        mine, other = (block.reshape(2, 2, -1, rank)[:, which] for block in (own_ab, got_ab))
        pair = jnp.stack([jnp.where(first, mine, other), jnp.where(first, other, mine)], 1)
        return pair.reshape(-1, rank)

    part_a, part_b = part_of(0), part_of(1)
    got_a = swap(part_a, "dp", high)
    got_b = swap(part_b, "dp", low)
    for turn in turns:
        turn.finish()
    work = gram.value
    rest = jnp.zeros_like(work)
    inverse = rest
    work, rest, inverse = cholesky_step(0, work, rest, inverse)
    work, rest, inverse = cholesky_step(1, work, rest, inverse)
    work, got_a, got_b, ring_c[1] = join(work, got_a, got_b, ring_c[1])
    part_a = in_order(part_a, got_a, "dp", high)
    part_b = in_order(part_b, got_b, "dp", low)
    got_a = swap(part_a, "dp", low)
    got_b = swap(part_b, "dp", high)
    ring_c.append(shifted(ring_c[1], "col"))
    work, rest, inverse = cholesky_step(2, work, rest, inverse)
    work, rest, inverse = cholesky_step(3, work, rest, inverse)
    inverse, ring_c[2] = join(inverse, ring_c[2])
    ring_c.append(shifted(ring_c[2], "col"))

    def old_rows(base, bit):
        return lax.dynamic_slice_in_dim(old_basis, base + bit * half, half, 0)

    def old_ring(back):
        return lax.dynamic_slice_in_dim(old_basis, (me_col + col_size - back) % col_size * quarter_c, quarter_c, 0)

    def basis(part):
        return contract(part, inverse, 1, 1, near).astype(jnp.bfloat16)

    basis_a, basis_b = basis(part_a), basis(part_b)
    basis_c = [basis(ring_c[0]), basis(ring_c[1]), basis(ring_c[2])]
    inner = contract(part_a, old_rows(base_a, at_low), 0, 0, near)
    inner = inner + contract(part_b, old_rows(base_b, at_high), 0, 0, near)
    for back in range(3):
        inner = inner + contract(ring_c[back], old_ring(back), 0, 0, near)
    got_a, got_b, ring_c[3], inner, basis_a, basis_b, basis_c = join(
        got_a, got_b, ring_c[3], inner, basis_a, basis_b, basis_c
    )
    inner = inner + contract(got_a, old_rows(base_a, 1 - at_low), 0, 0, near)
    inner = inner + contract(got_b, old_rows(base_b, 1 - at_high), 0, 0, near)
    inner = inner + contract(ring_c[3], old_ring(3), 0, 0, near)
    inner_got = swap(inner, "row", 0)
    basis_low = jnp.concatenate(basis_c + [basis(ring_c[3]), basis_a, basis(got_a), basis_b, basis(got_b)], 0)
    starts = [(me_col + col_size - back) % col_size * quarter_c for back in range(col_size)]
    starts += [base_a + at_low * half, base_a + (1 - at_low) * half]
    starts += [base_b + at_high * half, base_b + (1 - at_high) * half]
    starts = jnp.stack(starts).astype(jnp.int32)
    sizes = [quarter_c] * col_size + [half] * 4
    basis_low, inner_got = join(basis_low, inner_got)
    inner = inner + inner_got
    for bit in range(1, row_bits):
        inner = inner + swap(inner, "row", bit)
    correlation = contract(inverse, inner, 1, 0)
    place = me_dp * row_size + lax.axis_index("row")
    turner = jnp.where(place < group // 2, correlation, correlation * correlation)
    turned = jnp.concatenate([turn.result() for turn in turns], 1).reshape(rank, wide)
    turned = contract(turner, turned, 1, 0, near)
    turn = Exchange(turned.reshape(group, rank_dev, wide), [])
    turn.start_row()
    turn.got, basis_low = join(turn.got, basis_low)
    turn.finish()
    turns = turn.split(low, high)
    for turn in turns:
        turn.start()

    tile = cols // 7
    widths = [3 * tile, 4 * tile]

    def project(c):
        value = projection(starts, basis_low, grad, sizes, sum(widths[:c]), widths[c], tile)
        return Part(value.reshape((2,) * (dp_bits + row_bits) + (rank_dev, widths[c])), dp_bits, row_bits)

    front = project(0)
    front.value, basis_low, turns[0].got, turns[1].got = join(front.value, basis_low, turns[0].got, turns[1].got)
    front.start_row()
    for turn in turns:
        turn.finish()
        turn.start()
    back = project(1)
    back.value, front.got, turns[0].got, turns[1].got = join(back.value, front.got, turns[0].got, turns[1].got)
    front.finish()
    front = front.halves()
    for part, bit in zip(front, (low, high), strict=True):
        part.start("dp", bit)
    back.start_row()
    for turn in turns:
        turn.finish()
    front[0].got, front[1].got, back.got = join(front[0].got, front[1].got, back.got)
    back.finish()
    back = back.halves()
    for part, bit in zip(back, (low, high), strict=True):
        part.start("dp", bit)
    for part, bit in zip(front, (high, low), strict=True):
        part.finish()
        part.start("dp", bit)
    back[0].got, back[1].got, front[0].got, front[1].got = join(back[0].got, back[1].got, front[0].got, front[1].got)
    for part, bit in zip(back, (high, low), strict=True):
        part.finish()
        part.start("dp", bit)
    for part in front:
        part.finish()
    back[0].got, back[1].got = join(back[0].got, back[1].got)
    for part in back:
        part.finish()
    projected = jnp.concatenate([part.value.reshape(rank_dev, -1) for part in front + back], 1)
    turned = jnp.concatenate([turn.result() for turn in turns], 1).reshape(2, group // 2, rank_dev, wide)
    turned = turned.transpose(0, 2, 1, 3).reshape(2, rank_dev, cols)
    first_new = 0.9 * turned[0] + 0.1 * projected
    second_new = 0.95 * turned[1] + 0.05 * projected * projected
    return (projected, first_new, second_new)


def solution(mesh):
    in_specs = (
        P("dp", "row", "col"),
        P("col", None),
        P("row", None),
        P(("dp", "row"), "col"),
        P(("dp", "row"), "col"),
    )
    out_specs = (P(("dp", "row"), "col"), P(("dp", "row"), "col"), P(("dp", "row"), "col"))
    return jax.shard_map(local, mesh=mesh, in_specs=in_specs, out_specs=out_specs, check_vma=False)
```

```python
import functools

import jax
import jax.numpy as jnp
from jax import lax
from jax.experimental import pallas as pl
from jax.experimental.pallas import tpu as pltpu
from jax.sharding import PartitionSpec as P

highest = lax.Precision.HIGHEST
near = lax.Precision.HIGH
BLOCK = 128


def contract(a, b, a_dim, b_dim, precision=highest):
    return lax.dot_general(
        a, b, (((a_dim,), (b_dim,)), ((), ())), precision=precision, preferred_element_type=jnp.float32
    )


def eliminate(block, inverse_ref):
    groups = BLOCK // 8
    left = [block[8 * g : 8 * g + 8] for g in range(groups)]
    row_ids = lax.broadcasted_iota(jnp.int32, (8, BLOCK), 0)
    lane_ids = lax.broadcasted_iota(jnp.int32, (8, BLOCK), 1)
    right = [(lane_ids == row_ids + 8 * g).astype(jnp.float32) for g in range(groups)]
    for own in range(groups):
        at = 8 * own
        spread = {
            g: [jnp.broadcast_to(left[g][:, at + k : at + k + 1], (8, BLOCK)) for k in range(8)]
            for g in range(own, groups)
        }
        scaled = []
        for i in range(8):
            pivot = spread[own][i][i : i + 1]
            recip = 1.0 / pivot
            row, inv_row = left[own][i : i + 1], right[own][i : i + 1]
            inverse_ref[at + i : at + i + 1, :] = inv_row * lax.rsqrt(pivot)
            row, inv_row = row * recip, inv_row * recip
            scaled.append((row, inv_row))
            if i == 7:
                continue
            ratio = {k: spread[own][k][i : i + 1] * recip for k in range(i + 1, 8)}
            below = jnp.where(row_ids > i, spread[own][i], 0.0)
            left[own] = left[own] - below * row
            right[own] = right[own] - below * inv_row
            for g in range(own, groups):
                column = below if g == own else spread[g][i]
                for k in range(i + 1, 8):
                    spread[g][k] = spread[g][k] - column * ratio[k]
        for g in range(own + 1, groups):
            for i, (row, inv_row) in enumerate(scaled):
                left[g] = left[g] - spread[g][i] * row
                right[g] = right[g] - spread[g][i] * inv_row


def cholesky_kernel(index, work_in, rest_in, inverse_in, work_ref, rest_ref, inverse_ref, diag_ref):
    size = work_ref.shape[0]
    at = slice(index * BLOCK, (index + 1) * BLOCK)
    if index == 0:
        rows = lax.broadcasted_iota(jnp.int32, (size, size), 0)
        cols = lax.broadcasted_iota(jnp.int32, (size, size), 1)
        rest = (rows == cols).astype(jnp.float32)
    else:
        rest = rest_in[...]
        inverse_ref[...] = inverse_in[...]
    eliminate(work_in[at, at], diag_ref)
    diag = diag_ref[...]
    done = contract(diag, rest[at], 1, 0)
    inverse_ref[at, :] = done
    if index < size // BLOCK - 1:
        below = slice((index + 1) * BLOCK, size)
        factor = contract(work_in[below, at], diag, 1, 1)
        work_ref[below, below] = work_in[below, below] - contract(factor, factor, 1, 1)
        rest_ref[below, :] = rest[below] - contract(factor, done, 1, 0)


def cholesky_step(index, work, rest, inverse):
    size = work.shape[0]
    whole = jax.ShapeDtypeStruct((size, size), jnp.float32)
    spec = pl.BlockSpec(memory_space=pltpu.VMEM)
    return pl.pallas_call(
        functools.partial(cholesky_kernel, index),
        out_shape=[whole] * 3,
        in_specs=[spec] * 3,
        out_specs=[spec] * 3,
        scratch_shapes=[pltpu.VMEM((BLOCK, BLOCK), jnp.float32)],
        compiler_params=pltpu.CompilerParams(vmem_limit_bytes=32 << 20),
        cost_estimate=pl.CostEstimate(flops=1_000_000, bytes_accessed=100_000, transcendentals=0),
    )(work, rest, inverse)


def projection_kernel(sizes, first, tile, starts_ref, basis_ref, grad_ref, out_ref, held_ref, sems):
    step = pl.program_id(0)
    steps = pl.num_programs(0)

    def copies(index, slot):
        at = 0
        made = []
        for k, size in enumerate(sizes):
            source = grad_ref.at[
                pl.ds(pl.multiple_of(starts_ref[k], 16), size),
                pl.ds(pl.multiple_of(first + index * tile, 128), tile),
            ]
            made.append(pltpu.make_async_copy(source, held_ref.at[slot, pl.ds(at, size)], sems.at[slot, k]))
            at += size
        return made

    @pl.when(step == 0)
    def _():
        for copy in copies(0, 0):
            copy.start()

    @pl.when(step + 1 < steps)
    def _():
        for copy in copies(step + 1, (step + 1) % 2):
            copy.start()

    slot = step % 2
    for copy in copies(step, slot):
        copy.wait()
    out_ref[...] = lax.dot_general(
        basis_ref[...], held_ref[slot], (((0,), (0,)), ((), ())), preferred_element_type=jnp.float32
    )


def projection(starts, basis, grad, sizes, first, width, tile):
    rows, rank = basis.shape
    return pl.pallas_call(
        functools.partial(projection_kernel, sizes, first, tile),
        grid=(width // tile,),
        out_shape=jax.ShapeDtypeStruct((rank, width), jnp.float32),
        in_specs=[
            pl.BlockSpec(memory_space=pltpu.SMEM),
            pl.BlockSpec((rows, rank), lambda i: (0, 0), pipeline_mode=pl.Buffered(1)),
            pl.BlockSpec(memory_space=pl.ANY),
        ],
        out_specs=pl.BlockSpec((rank, tile), lambda i: (0, i)),
        scratch_shapes=[pltpu.VMEM((2, rows, tile), jnp.bfloat16), pltpu.SemaphoreType.DMA((2, len(sizes)))],
        compiler_params=pltpu.CompilerParams(vmem_limit_bytes=40 << 20),
        cost_estimate=pl.CostEstimate(flops=1_000_000, bytes_accessed=100_000, transcendentals=0),
    )(starts, basis, grad)


class Order:
    def __init__(self):
        self.mark = jnp.zeros((8, 128), jnp.float32)

    def __call__(self, *values):
        self.mark, *values = lax.optimization_barrier((self.mark,) + values)
        return values


def bits_of(axis):
    return lax.axis_size(axis).bit_length() - 1


def own_bit(axis, bit):
    return (lax.axis_index(axis) >> bit) & 1


def flipped(value, axis, mask):
    return lax.ppermute(value, axis, [(i, i ^ mask) for i in range(lax.axis_size(axis))])


def swap(value, axis, bit):
    return flipped(value, axis, 1 << bit)


def shifted(value, axis):
    size = lax.axis_size(axis)
    return lax.ppermute(value, axis, [(i, (i + 1) % size) for i in range(size)])


def split_half(value, axis, bit, dim=0):
    half = value.shape[dim] // 2
    me = own_bit(axis, bit)
    sent = lax.dynamic_slice_in_dim(value, (1 - me) * half, half, dim)
    kept = lax.dynamic_slice_in_dim(value, me * half, half, dim)
    return sent, kept


def in_order(value, other, axis, bit):
    first = own_bit(axis, bit) == 0
    return jnp.concatenate([jnp.where(first, value, other), jnp.where(first, other, value)], 0)


def scatter_sends(value, axis):
    me = lax.axis_index(axis)
    kept = lax.dynamic_index_in_dim(value, me, 0, keepdims=False)
    return kept, [
        lax.dynamic_index_in_dim(value, me ^ mask, 0, keepdims=False)
        for mask in range(1, lax.axis_size(axis))
    ]


def flip_all(sends, axis):
    return [flipped(send, axis, mask) for mask, send in enumerate(sends, 1)]


def copies_to_all(value, axis):
    return flip_all([value] * (lax.axis_size(axis) - 1), axis)


def placed(value, others, axis):
    me = lax.axis_index(axis)
    blocks = [value] + list(others)
    return jnp.stack(
        [lax.select_n(me, *[blocks[p ^ i] for i in range(len(blocks))]) for p in range(len(blocks))]
    )


def ring_placed(blocks, axis):
    me = lax.axis_index(axis)
    size = len(blocks)
    return jnp.concatenate(
        [lax.select_n(me, *[blocks[(i - p) % size] for i in range(size)]) for p in range(size)], 0
    )


class Sum:
    def __init__(self, value):
        self.value = value
        row = [("half", b) for b in range(bits_of("row"))]
        self.steps = row + [("scatter", "dp"), ("all", "col"), ("gather", "dp")]
        self.steps += [("double", b) for _, b in reversed(row)]

    def start(self):
        kind, what = self.steps[0]
        if kind == "half":
            sent, self.kept = split_half(self.value, "row", what)
            self.got = swap(sent, "row", what)
        elif kind == "double":
            self.got = swap(self.value, "row", what)
        elif kind == "scatter":
            size = lax.axis_size(what)
            self.kept, sends = scatter_sends(self.value.reshape((size, -1) + self.value.shape[1:]), what)
            self.got = flip_all(sends, what)
        else:
            self.got = copies_to_all(self.value, what)

    def finish(self):
        kind, what = self.steps.pop(0)
        if kind == "half":
            self.value = self.kept + self.got
        elif kind == "scatter":
            self.value = self.kept + sum(self.got)
        elif kind == "all":
            self.value = placed(self.value, self.got, what).sum(0)
        elif kind == "double":
            self.value = in_order(self.value, self.got, "row", what)
        else:
            self.value = placed(self.value, self.got, what).reshape((-1,) + self.value.shape[1:])


class Exchange:
    def __init__(self, value, dp_order, row=True):
        self.tail = value.shape[1:]
        dp_bits, row_bits = bits_of("dp"), bits_of("row")
        self.bits = [("dp", b) for b in reversed(range(dp_bits))] + [("row", b) for b in reversed(range(row_bits))]
        self.value = value.reshape((2,) * len(self.bits) + self.tail)
        self.left = [("row", b) for b in range(row_bits) if row] + [("dp", b) for b in dp_order]

    def start(self):
        axis, bit = self.left[0]
        place = self.bits.index((axis, bit))
        me = own_bit(axis, bit)
        sent = lax.dynamic_index_in_dim(self.value, 1 - me, place, keepdims=True)
        self.kept = lax.dynamic_index_in_dim(self.value, me, place, keepdims=True)
        self.got = swap(sent, axis, bit)

    def finish(self):
        axis, bit = self.left.pop(0)
        place = self.bits.index((axis, bit))
        me = own_bit(axis, bit)
        kept, got = self.kept, self.got
        self.value = jnp.concatenate([jnp.where(me == 0, kept, got), jnp.where(me == 0, got, kept)], place)

    def start_row(self):
        while len(self.left) > 1 and self.left[1][0] == "row":
            self.start()
            self.finish()
        self.start()

    def split(self, low, high):
        half = self.tail[0] // 2
        return [
            Exchange(self.result()[:, at : at + half], order, False)
            for at, order in ((0, [low, high]), (half, [high, low]))
        ]

    def result(self):
        return self.value.reshape((1 << len(self.bits),) + self.tail)


def lower_blocks(square):
    count = square.shape[0] // BLOCK
    return [
        square[i * BLOCK : (i + 1) * BLOCK, k * BLOCK : (k + 1) * BLOCK] for i in range(count) for k in range(i + 1)
    ]


def from_lower_blocks(stacked, size):
    count = size // BLOCK
    rows = []
    at = 0
    for i in range(count):
        blocks = [stacked[at + k * BLOCK : at + (k + 1) * BLOCK] for k in range(i + 1)]
        at += (i + 1) * BLOCK
        rows.append(jnp.concatenate(blocks + [jnp.zeros_like(blocks[0])] * (count - 1 - i), 1))
    return jnp.concatenate(rows, 0)


class Part:
    def __init__(self, value, dp_bits, row_bits):
        self.value = value
        self.bits = (dp_bits, row_bits)

    def start(self, axis, bit):
        dp_bits, row_bits = self.bits
        place = dp_bits - 1 - bit if axis == "dp" else dp_bits + row_bits - 1 - bit
        sent, self.kept = split_half(self.value, axis, bit, place)
        self.got = swap(sent, axis, bit)

    def finish(self):
        self.value = self.kept + self.got

    def start_row(self):
        for bit in range(self.bits[1]):
            if bit > 0:
                self.finish()
            self.start("row", bit)

    def halves(self):
        cut = self.value.shape[-1] // 2
        return [Part(self.value[..., :cut], *self.bits), Part(self.value[..., cut:], *self.bits)]


def local(gradients, test_matrix, old_basis, first_moment, second_moment):
    join = Order()
    grad = gradients[0]
    rows, cols = grad.shape
    rank_dev = first_moment.shape[0]
    dp_size, row_size, col_size = (lax.axis_size(a) for a in ("dp", "row", "col"))
    group = dp_size * row_size
    rank = rank_dev * group
    wide = 2 * cols // group
    dp_bits, row_bits = bits_of("dp"), bits_of("row")
    low, high = 0, dp_bits - 1
    me_col, me_dp = lax.axis_index("col"), lax.axis_index("dp")
    at_low, at_high = own_bit("dp", low), own_bit("dp", high)

    test_values = test_matrix.astype(jnp.bfloat16)
    unit = rows // 32
    size_c, size = 10 * unit, 11 * unit
    base_a, base_b = size_c, size_c + size
    quarter_c = size_c // col_size
    half = size // 2

    both = jnp.concatenate([first_moment, second_moment], 1).reshape(rank_dev, group, wide).transpose(1, 0, 2)
    turn = Exchange(both, [])
    turn.start_row()
    whole = jnp.dot(grad, test_values, preferred_element_type=jnp.float32)
    whole, turn.got = join(whole, turn.got)

    def block_c(back):
        return lax.dynamic_slice_in_dim(whole, (me_col + 2 * col_size - back) % col_size * quarter_c, quarter_c, 0)

    got_a = swap(lax.dynamic_slice_in_dim(whole, base_a + (1 - at_low) * half, half, 0), "dp", low)
    got_b = swap(lax.dynamic_slice_in_dim(whole, base_b + (1 - at_high) * half, half, 0), "dp", high)
    ring = shifted(block_c(1), "col")
    (ring,) = join(ring)
    ring = shifted(ring + block_c(2), "col")
    turn.finish()
    turns = turn.split(low, high)
    got_a, got_b = join(got_a, got_b)
    kept_a = lax.dynamic_slice_in_dim(whole, base_a + at_low * half, half, 0)
    kept_b = lax.dynamic_slice_in_dim(whole, base_b + at_high * half, half, 0)
    sent_a, kept_a = split_half(kept_a + got_a, "dp", high)
    sent_b, kept_b = split_half(kept_b + got_b, "dp", low)
    got_a = swap(sent_a, "dp", high)
    got_b = swap(sent_b, "dp", low)
    (ring,) = join(ring)
    ring = shifted(ring + block_c(3), "col")
    got_a, got_b = join(got_a, got_b)
    part_ab = jnp.concatenate(
        [(kept_a + got_a).reshape(col_size, -1, rank), (kept_b + got_b).reshape(col_size, -1, rank)], 1
    ).reshape(2, 2, -1, rank)
    sent_ab, kept_ab = split_half(part_ab, "col", 0, 1)
    got_ab = swap(sent_ab, "col", 0)
    for turn in turns:
        turn.start()
    (ring,) = join(ring)
    sent_c, kept_c = split_half(ring + block_c(4), "dp", low)
    got_c = swap(sent_c, "dp", low)
    got_ab, got_c, turns[0].got, turns[1].got = join(got_ab, got_c, turns[0].got, turns[1].got)
    sent_ab, kept_ab = split_half(kept_ab + got_ab, "col", 1, 0)
    sent_ab, turns[0].got, turns[1].got, got_c = join(sent_ab, turns[0].got, turns[1].got, got_c)
    got_ab = swap(sent_ab, "col", 1)
    sent_c, kept_c = split_half(kept_c + got_c, "dp", high)
    got_c = swap(sent_c, "dp", high)
    for turn in turns:
        turn.finish()
        turn.start()
    got_ab, got_c, turns[0].got, turns[1].got = join(got_ab, got_c, turns[0].got, turns[1].got)
    own_ab = (kept_ab + got_ab).reshape(-1, rank)
    own_c = kept_c + got_c

    got_ab = swap(own_ab, "col", 1)
    got_c = swap(own_c, "dp", high)
    own = jnp.concatenate([own_ab, own_c], 0)
    gram = Sum(jnp.concatenate(lower_blocks(contract(own, own, 0, 0)), 0))
    for _ in range(row_bits - 1):
        gram.start()
        (gram.got,) = join(gram.got)
        gram.finish()
    gram.start()
    gram.got, got_c = join(gram.got, got_c)
    gram.finish()
    own_c = in_order(own_c, got_c, "dp", high)
    gram.start()
    got_c = swap(own_c, "dp", low)
    gram.got, got_c, got_ab = join(gram.got, got_c, got_ab)
    gram.finish()
    gram.start()
    own_ab = in_order(own_ab, got_ab, "col", 1)
    got_ab = swap(own_ab, "col", 0)
    (gram.got,) = join(gram.got)
    gram.finish()
    gram.start()
    ring_c = [in_order(own_c, got_c, "dp", low)]
    ring_c.append(shifted(ring_c[0], "col"))
    (gram.got,) = join(gram.got)
    gram.finish()
    for _ in range(row_bits):
        gram.start()
        (gram.got,) = join(gram.got)
        gram.finish()
    (got_ab,) = join(got_ab)

    def part_of(which):
        first = own_bit("col", 0) == 0
        mine, other = (block.reshape(2, 2, -1, rank)[:, which] for block in (own_ab, got_ab))
        pair = jnp.stack([jnp.where(first, mine, other), jnp.where(first, other, mine)], 1)
        return pair.reshape(-1, rank)

    part_a, part_b = part_of(0), part_of(1)
    got_a = swap(part_a, "dp", high)
    got_b = swap(part_b, "dp", low)
    for turn in turns:
        turn.finish()
    work = from_lower_blocks(gram.value, rank)
    rest = jnp.zeros_like(work)
    inverse = rest
    work, rest, inverse = cholesky_step(0, work, rest, inverse)
    work, rest, inverse = cholesky_step(1, work, rest, inverse)
    work, got_a, got_b, ring_c[1] = join(work, got_a, got_b, ring_c[1])
    part_a = in_order(part_a, got_a, "dp", high)
    part_b = in_order(part_b, got_b, "dp", low)
    got_a = swap(part_a, "dp", low)
    got_b = swap(part_b, "dp", high)
    ring_c.append(shifted(ring_c[1], "col"))
    work, rest, inverse = cholesky_step(2, work, rest, inverse)
    work, rest, inverse = cholesky_step(3, work, rest, inverse)
    inverse, ring_c[2] = join(inverse, ring_c[2])
    ring_c.append(shifted(ring_c[2], "col"))

    def old_rows(base, bit):
        return lax.dynamic_slice_in_dim(old_basis, base + bit * half, half, 0)

    def old_ring(back):
        return lax.dynamic_slice_in_dim(old_basis, (me_col + col_size - back) % col_size * quarter_c, quarter_c, 0)

    def basis(part):
        return contract(part, inverse, 1, 1, near).astype(jnp.bfloat16)

    basis_a, basis_b = basis(part_a), basis(part_b)
    basis_c = [basis(ring_c[0]), basis(ring_c[1]), basis(ring_c[2])]
    inner = contract(part_a, old_rows(base_a, at_low), 0, 0, near)
    inner = inner + contract(part_b, old_rows(base_b, at_high), 0, 0, near)
    for back in range(3):
        inner = inner + contract(ring_c[back], old_ring(back), 0, 0, near)
    got_a, got_b, ring_c[3], inner, basis_a, basis_b, basis_c = join(
        got_a, got_b, ring_c[3], inner, basis_a, basis_b, basis_c
    )
    inner = inner + contract(got_a, old_rows(base_a, 1 - at_low), 0, 0, near)
    inner = inner + contract(got_b, old_rows(base_b, 1 - at_high), 0, 0, near)
    inner = inner + contract(ring_c[3], old_ring(3), 0, 0, near)
    inner_got = swap(inner, "row", 0)
    basis_low = jnp.concatenate(basis_c + [basis(ring_c[3]), basis_a, basis(got_a), basis_b, basis(got_b)], 0)
    starts = [(me_col + col_size - back) % col_size * quarter_c for back in range(col_size)]
    starts += [base_a + at_low * half, base_a + (1 - at_low) * half]
    starts += [base_b + at_high * half, base_b + (1 - at_high) * half]
    starts = jnp.stack(starts).astype(jnp.int32)
    sizes = [quarter_c] * col_size + [half] * 4
    basis_low, inner_got = join(basis_low, inner_got)
    inner = inner + inner_got
    for bit in range(1, row_bits):
        inner = inner + swap(inner, "row", bit)
    correlation = contract(inverse, inner, 1, 0, near)
    place = me_dp * row_size + lax.axis_index("row")
    turner = jnp.where(place < group // 2, correlation, correlation * correlation)
    turned = jnp.concatenate([turn.result() for turn in turns], 1).reshape(rank, wide)
    turned = contract(turner, turned, 1, 0, near)
    turn = Exchange(turned.reshape(group, rank_dev, wide), [])
    turn.start_row()
    turn.got, basis_low = join(turn.got, basis_low)
    turn.finish()
    turns = turn.split(low, high)
    for turn in turns:
        turn.start()

    tile = cols // 7
    widths = [3 * tile, 4 * tile]

    def project(c):
        value = projection(starts, basis_low, grad, sizes, sum(widths[:c]), widths[c], tile)
        return Part(value.reshape((2,) * (dp_bits + row_bits) + (rank_dev, widths[c])), dp_bits, row_bits)

    front = project(0)
    front.value, basis_low, turns[0].got, turns[1].got = join(front.value, basis_low, turns[0].got, turns[1].got)
    front.start_row()
    for turn in turns:
        turn.finish()
        turn.start()
    back = project(1)
    back.value, front.got, turns[0].got, turns[1].got = join(back.value, front.got, turns[0].got, turns[1].got)
    front.finish()
    front = front.halves()
    for part, bit in zip(front, (low, high), strict=True):
        part.start("dp", bit)
    back.start_row()
    for turn in turns:
        turn.finish()
    front[0].got, front[1].got, back.got = join(front[0].got, front[1].got, back.got)
    back.finish()
    back = back.halves()
    for part, bit in zip(back, (low, high), strict=True):
        part.start("dp", bit)
    for part, bit in zip(front, (high, low), strict=True):
        part.finish()
        part.start("dp", bit)
    back[0].got, back[1].got, front[0].got, front[1].got = join(back[0].got, back[1].got, front[0].got, front[1].got)
    for part, bit in zip(back, (high, low), strict=True):
        part.finish()
        part.start("dp", bit)
    for part in front:
        part.finish()
    back[0].got, back[1].got = join(back[0].got, back[1].got)
    for part in back:
        part.finish()
    projected = jnp.concatenate([part.value.reshape(rank_dev, -1) for part in front + back], 1)
    turned = jnp.concatenate([turn.result() for turn in turns], 1).reshape(2, group // 2, rank_dev, wide)
    turned = turned.transpose(0, 2, 1, 3).reshape(2, rank_dev, cols)
    first_new = 0.9 * turned[0] + 0.1 * projected
    second_new = 0.95 * turned[1] + 0.05 * projected * projected
    return (projected, first_new, second_new)


def solution(mesh):
    in_specs = (
        P("dp", "row", "col"),
        P("col", None),
        P("row", None),
        P(("dp", "row"), "col"),
        P(("dp", "row"), "col"),
    )
    out_specs = (P(("dp", "row"), "col"), P(("dp", "row"), "col"), P(("dp", "row"), "col"))
    return jax.shard_map(local, mesh=mesh, in_specs=in_specs, out_specs=out_specs, check_vma=False)
```

```python
import functools

import jax
import jax.numpy as jnp
from jax import lax
from jax.experimental import pallas as pl
from jax.experimental.pallas import tpu as pltpu
from jax.sharding import PartitionSpec as P

highest = lax.Precision.HIGHEST
near = lax.Precision.HIGH
BLOCK = 128


def contract(a, b, a_dim, b_dim, precision=highest):
    return lax.dot_general(
        a, b, (((a_dim,), (b_dim,)), ((), ())), precision=precision, preferred_element_type=jnp.float32
    )


def eliminate(block, inverse_ref):
    groups = BLOCK // 8
    left = [block[8 * g : 8 * g + 8] for g in range(groups)]
    row_ids = lax.broadcasted_iota(jnp.int32, (8, BLOCK), 0)
    lane_ids = lax.broadcasted_iota(jnp.int32, (8, BLOCK), 1)
    right = [(lane_ids == row_ids + 8 * g).astype(jnp.float32) for g in range(groups)]
    for own in range(groups):
        at = 8 * own
        spread = {
            g: [jnp.broadcast_to(left[g][:, at + k : at + k + 1], (8, BLOCK)) for k in range(8)]
            for g in range(own, groups)
        }
        scaled = []
        for i in range(8):
            pivot = spread[own][i][i : i + 1]
            recip = 1.0 / pivot
            row, inv_row = left[own][i : i + 1], right[own][i : i + 1]
            inverse_ref[at + i : at + i + 1, :] = inv_row * lax.rsqrt(pivot)
            row, inv_row = row * recip, inv_row * recip
            scaled.append((row, inv_row))
            if i == 7:
                continue
            ratio = {k: spread[own][k][i : i + 1] * recip for k in range(i + 1, 8)}
            below = jnp.where(row_ids > i, spread[own][i], 0.0)
            left[own] = left[own] - below * row
            right[own] = right[own] - below * inv_row
            for g in range(own, groups):
                column = below if g == own else spread[g][i]
                for k in range(i + 1, 8):
                    spread[g][k] = spread[g][k] - column * ratio[k]
        for g in range(own + 1, groups):
            for i, (row, inv_row) in enumerate(scaled):
                left[g] = left[g] - spread[g][i] * row
                right[g] = right[g] - spread[g][i] * inv_row


def cholesky_kernel(index, work_in, rest_in, inverse_in, work_ref, rest_ref, inverse_ref, diag_ref):
    size = work_ref.shape[0]
    at = slice(index * BLOCK, (index + 1) * BLOCK)
    if index == 0:
        rows = lax.broadcasted_iota(jnp.int32, (size, size), 0)
        cols = lax.broadcasted_iota(jnp.int32, (size, size), 1)
        rest = (rows == cols).astype(jnp.float32)
    else:
        rest = rest_in[...]
        inverse_ref[...] = inverse_in[...]
    eliminate(work_in[at, at], diag_ref)
    diag = diag_ref[...]
    done = contract(diag, rest[at], 1, 0)
    inverse_ref[at, :] = done
    if index < size // BLOCK - 1:
        below = slice((index + 1) * BLOCK, size)
        factor = contract(work_in[below, at], diag, 1, 1)
        work_ref[below, below] = work_in[below, below] - contract(factor, factor, 1, 1)
        rest_ref[below, :] = rest[below] - contract(factor, done, 1, 0)


def cholesky_step(index, work, rest, inverse):
    size = work.shape[0]
    whole = jax.ShapeDtypeStruct((size, size), jnp.float32)
    spec = pl.BlockSpec(memory_space=pltpu.VMEM)
    return pl.pallas_call(
        functools.partial(cholesky_kernel, index),
        out_shape=[whole] * 3,
        in_specs=[spec] * 3,
        out_specs=[spec] * 3,
        scratch_shapes=[pltpu.VMEM((BLOCK, BLOCK), jnp.float32)],
        compiler_params=pltpu.CompilerParams(vmem_limit_bytes=32 << 20),
        cost_estimate=pl.CostEstimate(flops=1_000_000, bytes_accessed=100_000, transcendentals=0),
    )(work, rest, inverse)


def projection_kernel(sizes, first, tile, starts_ref, basis_ref, grad_ref, out_ref, held_ref, sems):
    step = pl.program_id(0)
    steps = pl.num_programs(0)

    def copies(index, slot):
        at = 0
        made = []
        for k, size in enumerate(sizes):
            source = grad_ref.at[
                pl.ds(pl.multiple_of(starts_ref[k], 16), size),
                pl.ds(pl.multiple_of(first + index * tile, 128), tile),
            ]
            made.append(pltpu.make_async_copy(source, held_ref.at[slot, pl.ds(at, size)], sems.at[slot, k]))
            at += size
        return made

    @pl.when(step == 0)
    def _():
        for copy in copies(0, 0):
            copy.start()

    @pl.when(step + 1 < steps)
    def _():
        for copy in copies(step + 1, (step + 1) % 2):
            copy.start()

    slot = step % 2
    for copy in copies(step, slot):
        copy.wait()
    out_ref[...] = lax.dot_general(
        basis_ref[...], held_ref[slot], (((0,), (0,)), ((), ())), preferred_element_type=jnp.float32
    )


def projection(starts, basis, grad, sizes, first, width, tile):
    rows, rank = basis.shape
    return pl.pallas_call(
        functools.partial(projection_kernel, sizes, first, tile),
        grid=(width // tile,),
        out_shape=jax.ShapeDtypeStruct((rank, width), jnp.float32),
        in_specs=[
            pl.BlockSpec(memory_space=pltpu.SMEM),
            pl.BlockSpec((rows, rank), lambda i: (0, 0), pipeline_mode=pl.Buffered(1)),
            pl.BlockSpec(memory_space=pl.ANY),
        ],
        out_specs=pl.BlockSpec((rank, tile), lambda i: (0, i)),
        scratch_shapes=[pltpu.VMEM((2, rows, tile), jnp.bfloat16), pltpu.SemaphoreType.DMA((2, len(sizes)))],
        compiler_params=pltpu.CompilerParams(vmem_limit_bytes=40 << 20),
        cost_estimate=pl.CostEstimate(flops=1_000_000, bytes_accessed=100_000, transcendentals=0),
    )(starts, basis, grad)


class Order:
    def __init__(self):
        self.mark = jnp.zeros((8, 128), jnp.float32)

    def __call__(self, *values):
        self.mark, *values = lax.optimization_barrier((self.mark,) + values)
        return values


def bits_of(axis):
    return lax.axis_size(axis).bit_length() - 1


def own_bit(axis, bit):
    return (lax.axis_index(axis) >> bit) & 1


def flipped(value, axis, mask):
    return lax.ppermute(value, axis, [(i, i ^ mask) for i in range(lax.axis_size(axis))])


def swap(value, axis, bit):
    return flipped(value, axis, 1 << bit)


def shifted(value, axis):
    size = lax.axis_size(axis)
    return lax.ppermute(value, axis, [(i, (i + 1) % size) for i in range(size)])


def split_half(value, axis, bit, dim=0):
    half = value.shape[dim] // 2
    me = own_bit(axis, bit)
    sent = lax.dynamic_slice_in_dim(value, (1 - me) * half, half, dim)
    kept = lax.dynamic_slice_in_dim(value, me * half, half, dim)
    return sent, kept


def in_order(value, other, axis, bit):
    first = own_bit(axis, bit) == 0
    return jnp.concatenate([jnp.where(first, value, other), jnp.where(first, other, value)], 0)


def scatter_sends(value, axis):
    me = lax.axis_index(axis)
    kept = lax.dynamic_index_in_dim(value, me, 0, keepdims=False)
    return kept, [
        lax.dynamic_index_in_dim(value, me ^ mask, 0, keepdims=False)
        for mask in range(1, lax.axis_size(axis))
    ]


def flip_all(sends, axis):
    return [flipped(send, axis, mask) for mask, send in enumerate(sends, 1)]


def copies_to_all(value, axis):
    return flip_all([value] * (lax.axis_size(axis) - 1), axis)


def placed(value, others, axis):
    me = lax.axis_index(axis)
    blocks = [value] + list(others)
    return jnp.stack(
        [lax.select_n(me, *[blocks[p ^ i] for i in range(len(blocks))]) for p in range(len(blocks))]
    )


def ring_placed(blocks, axis):
    me = lax.axis_index(axis)
    size = len(blocks)
    return jnp.concatenate(
        [lax.select_n(me, *[blocks[(i - p) % size] for i in range(size)]) for p in range(size)], 0
    )


class Sum:
    def __init__(self, value):
        self.value = value
        row = [("half", b) for b in range(bits_of("row"))]
        self.steps = row + [("scatter", "dp"), ("all", "col"), ("gather", "dp")]
        self.steps += [("double", b) for _, b in reversed(row)]

    def start(self):
        kind, what = self.steps[0]
        if kind == "half":
            sent, self.kept = split_half(self.value, "row", what)
            self.got = swap(sent, "row", what)
        elif kind == "double":
            self.got = swap(self.value, "row", what)
        elif kind == "scatter":
            size = lax.axis_size(what)
            self.kept, sends = scatter_sends(self.value.reshape((size, -1) + self.value.shape[1:]), what)
            self.got = flip_all(sends, what)
        else:
            self.got = copies_to_all(self.value, what)

    def finish(self):
        kind, what = self.steps.pop(0)
        if kind == "half":
            self.value = self.kept + self.got
        elif kind == "scatter":
            self.value = self.kept + sum(self.got)
        elif kind == "all":
            self.value = placed(self.value, self.got, what).sum(0)
        elif kind == "double":
            self.value = in_order(self.value, self.got, "row", what)
        else:
            self.value = placed(self.value, self.got, what).reshape((-1,) + self.value.shape[1:])


class Exchange:
    def __init__(self, value, dp_order, row=True):
        self.tail = value.shape[1:]
        dp_bits, row_bits = bits_of("dp"), bits_of("row")
        self.bits = [("dp", b) for b in reversed(range(dp_bits))] + [("row", b) for b in reversed(range(row_bits))]
        self.value = value.reshape((2,) * len(self.bits) + self.tail)
        self.left = [("row", b) for b in range(row_bits) if row] + [("dp", b) for b in dp_order]

    def start(self):
        axis, bit = self.left[0]
        place = self.bits.index((axis, bit))
        me = own_bit(axis, bit)
        sent = lax.dynamic_index_in_dim(self.value, 1 - me, place, keepdims=True)
        self.kept = lax.dynamic_index_in_dim(self.value, me, place, keepdims=True)
        self.got = swap(sent, axis, bit)

    def finish(self):
        axis, bit = self.left.pop(0)
        place = self.bits.index((axis, bit))
        me = own_bit(axis, bit)
        kept, got = self.kept, self.got
        self.value = jnp.concatenate([jnp.where(me == 0, kept, got), jnp.where(me == 0, got, kept)], place)

    def start_row(self):
        while len(self.left) > 1 and self.left[1][0] == "row":
            self.start()
            self.finish()
        self.start()

    def split(self, low, high):
        half = self.tail[0] // 2
        return [
            Exchange(self.result()[:, at : at + half], order, False)
            for at, order in ((0, [low, high]), (half, [high, low]))
        ]

    def result(self):
        return self.value.reshape((1 << len(self.bits),) + self.tail)


def lower_blocks(square):
    count = square.shape[0] // BLOCK
    return [
        square[i * BLOCK : (i + 1) * BLOCK, k * BLOCK : (k + 1) * BLOCK] for i in range(count) for k in range(i + 1)
    ]


def from_lower_blocks(stacked, size):
    count = size // BLOCK
    rows = []
    at = 0
    for i in range(count):
        blocks = [stacked[at + k * BLOCK : at + (k + 1) * BLOCK] for k in range(i + 1)]
        at += (i + 1) * BLOCK
        rows.append(jnp.concatenate(blocks + [jnp.zeros_like(blocks[0])] * (count - 1 - i), 1))
    return jnp.concatenate(rows, 0)


class Part:
    def __init__(self, value, dp_bits, row_bits):
        self.value = value
        self.bits = (dp_bits, row_bits)

    def start(self, axis, bit):
        dp_bits, row_bits = self.bits
        place = dp_bits - 1 - bit if axis == "dp" else dp_bits + row_bits - 1 - bit
        sent, self.kept = split_half(self.value, axis, bit, place)
        self.got = swap(sent, axis, bit)

    def finish(self):
        self.value = self.kept + self.got

    def start_row(self):
        for bit in range(self.bits[1]):
            if bit > 0:
                self.finish()
            self.start("row", bit)

    def halves(self):
        cut = self.value.shape[-1] // 2
        return [Part(self.value[..., :cut], *self.bits), Part(self.value[..., cut:], *self.bits)]


def local(gradients, test_matrix, old_basis, first_moment, second_moment):
    join = Order()
    grad = gradients[0]
    rows, cols = grad.shape
    rank_dev = first_moment.shape[0]
    dp_size, row_size, col_size = (lax.axis_size(a) for a in ("dp", "row", "col"))
    group = dp_size * row_size
    rank = rank_dev * group
    wide = 2 * cols // group
    dp_bits, row_bits = bits_of("dp"), bits_of("row")
    low, high = 0, dp_bits - 1
    me_col, me_dp = lax.axis_index("col"), lax.axis_index("dp")
    at_low, at_high = own_bit("dp", low), own_bit("dp", high)

    test_values = test_matrix.astype(jnp.bfloat16)
    unit = rows // 32
    size_c, size = 10 * unit, 11 * unit
    base_a, base_b = size_c, size_c + size
    quarter_c = size_c // col_size
    half = size // 2

    both = jnp.concatenate([first_moment, second_moment], 1).reshape(rank_dev, group, wide).transpose(1, 0, 2)
    turn = Exchange(both, [])
    turn.start_row()
    whole = jnp.dot(grad, test_values, preferred_element_type=jnp.float32)
    whole, turn.got = join(whole, turn.got)

    def block_c(back):
        return lax.dynamic_slice_in_dim(whole, (me_col + 2 * col_size - back) % col_size * quarter_c, quarter_c, 0)

    got_a = swap(lax.dynamic_slice_in_dim(whole, base_a + (1 - at_low) * half, half, 0), "dp", low)
    got_b = swap(lax.dynamic_slice_in_dim(whole, base_b + (1 - at_high) * half, half, 0), "dp", high)
    ring = shifted(block_c(1), "col")
    (ring,) = join(ring)
    ring = shifted(ring + block_c(2), "col")
    turn.finish()
    turns = turn.split(low, high)
    got_a, got_b = join(got_a, got_b)
    kept_a = lax.dynamic_slice_in_dim(whole, base_a + at_low * half, half, 0)
    kept_b = lax.dynamic_slice_in_dim(whole, base_b + at_high * half, half, 0)
    sent_a, kept_a = split_half(kept_a + got_a, "dp", high)
    sent_b, kept_b = split_half(kept_b + got_b, "dp", low)
    got_a = swap(sent_a, "dp", high)
    got_b = swap(sent_b, "dp", low)
    (ring,) = join(ring)
    ring = shifted(ring + block_c(3), "col")
    got_a, got_b = join(got_a, got_b)
    part_ab = jnp.concatenate(
        [(kept_a + got_a).reshape(col_size, -1, rank), (kept_b + got_b).reshape(col_size, -1, rank)], 1
    ).reshape(2, 2, -1, rank)
    sent_ab, kept_ab = split_half(part_ab, "col", 0, 1)
    got_ab = swap(sent_ab, "col", 0)
    for turn in turns:
        turn.start()
    (ring,) = join(ring)
    sent_c, kept_c = split_half(ring + block_c(4), "dp", low)
    got_c = swap(sent_c, "dp", low)
    got_ab, got_c, turns[0].got, turns[1].got = join(got_ab, got_c, turns[0].got, turns[1].got)
    sent_ab, kept_ab = split_half(kept_ab + got_ab, "col", 1, 0)
    sent_ab, turns[0].got, turns[1].got, got_c = join(sent_ab, turns[0].got, turns[1].got, got_c)
    got_ab = swap(sent_ab, "col", 1)
    sent_c, kept_c = split_half(kept_c + got_c, "dp", high)
    got_c = swap(sent_c, "dp", high)
    for turn in turns:
        turn.finish()
        turn.start()
    got_ab, got_c, turns[0].got, turns[1].got = join(got_ab, got_c, turns[0].got, turns[1].got)
    own_ab = (kept_ab + got_ab).reshape(-1, rank)
    own_c = kept_c + got_c

    got_ab = swap(own_ab, "col", 1)
    got_c = swap(own_c, "dp", high)
    own = jnp.concatenate([own_ab, own_c], 0)
    gram = Sum(jnp.concatenate(lower_blocks(contract(own, own, 0, 0)), 0))
    for _ in range(row_bits - 1):
        gram.start()
        (gram.got,) = join(gram.got)
        gram.finish()
    gram.start()
    gram.got, got_c = join(gram.got, got_c)
    gram.finish()
    own_c = in_order(own_c, got_c, "dp", high)
    gram.start()
    got_c = swap(own_c, "dp", low)
    gram.got, got_c, got_ab = join(gram.got, got_c, got_ab)
    gram.finish()
    gram.start()
    own_ab = in_order(own_ab, got_ab, "col", 1)
    got_ab = swap(own_ab, "col", 0)
    (gram.got,) = join(gram.got)
    gram.finish()
    gram.start()
    ring_c = [in_order(own_c, got_c, "dp", low)]
    ring_c.append(shifted(ring_c[0], "col"))
    (gram.got,) = join(gram.got)
    gram.finish()
    for _ in range(row_bits):
        gram.start()
        (gram.got,) = join(gram.got)
        gram.finish()
    (got_ab,) = join(got_ab)

    def part_of(which):
        first = own_bit("col", 0) == 0
        mine, other = (block.reshape(2, 2, -1, rank)[:, which] for block in (own_ab, got_ab))
        pair = jnp.stack([jnp.where(first, mine, other), jnp.where(first, other, mine)], 1)
        return pair.reshape(-1, rank)

    part_a, part_b = part_of(0), part_of(1)
    got_a = swap(part_a, "dp", high)
    got_b = swap(part_b, "dp", low)
    for turn in turns:
        turn.finish()
    work = from_lower_blocks(gram.value, rank)
    rest = jnp.zeros_like(work)
    inverse = rest
    work, rest, inverse = cholesky_step(0, work, rest, inverse)
    work, rest, inverse = cholesky_step(1, work, rest, inverse)
    work, got_a, got_b, ring_c[1] = join(work, got_a, got_b, ring_c[1])
    part_a = in_order(part_a, got_a, "dp", high)
    part_b = in_order(part_b, got_b, "dp", low)
    got_a = swap(part_a, "dp", low)
    got_b = swap(part_b, "dp", high)
    ring_c.append(shifted(ring_c[1], "col"))
    work, rest, inverse = cholesky_step(2, work, rest, inverse)
    work, rest, inverse = cholesky_step(3, work, rest, inverse)
    inverse, ring_c[2] = join(inverse, ring_c[2])
    ring_c.append(shifted(ring_c[2], "col"))

    def old_rows(base, bit):
        return lax.dynamic_slice_in_dim(old_basis, base + bit * half, half, 0)

    def old_ring(back):
        return lax.dynamic_slice_in_dim(old_basis, (me_col + col_size - back) % col_size * quarter_c, quarter_c, 0)

    def basis(part):
        return contract(part, inverse, 1, 1, near).astype(jnp.bfloat16)

    basis_a, basis_b = basis(part_a), basis(part_b)
    basis_c = [basis(ring_c[0]), basis(ring_c[1]), basis(ring_c[2])]
    inner = contract(part_a, old_rows(base_a, at_low), 0, 0, near)
    inner = inner + contract(part_b, old_rows(base_b, at_high), 0, 0, near)
    for back in range(3):
        inner = inner + contract(ring_c[back], old_ring(back), 0, 0, near)
    got_a, got_b, ring_c[3], inner, basis_a, basis_b, basis_c = join(
        got_a, got_b, ring_c[3], inner, basis_a, basis_b, basis_c
    )
    inner = inner + contract(got_a, old_rows(base_a, 1 - at_low), 0, 0, near)
    inner = inner + contract(got_b, old_rows(base_b, 1 - at_high), 0, 0, near)
    inner = inner + contract(ring_c[3], old_ring(3), 0, 0, near)
    inner_got = swap(inner, "row", 0)
    basis_low = jnp.concatenate(basis_c + [basis(ring_c[3]), basis_a, basis(got_a), basis_b, basis(got_b)], 0)
    starts = [(me_col + col_size - back) % col_size * quarter_c for back in range(col_size)]
    starts += [base_a + at_low * half, base_a + (1 - at_low) * half]
    starts += [base_b + at_high * half, base_b + (1 - at_high) * half]
    starts = jnp.stack(starts).astype(jnp.int32)
    sizes = [quarter_c] * col_size + [half] * 4
    basis_low, inner_got = join(basis_low, inner_got)
    inner = inner + inner_got
    for bit in range(1, row_bits):
        inner = inner + swap(inner, "row", bit)
    correlation = contract(inverse, inner, 1, 0, near)
    place = me_dp * row_size + lax.axis_index("row")
    turner = jnp.where(place < group // 2, correlation, correlation * correlation)
    turned = jnp.concatenate([turn.result() for turn in turns], 1).reshape(rank, wide)
    turned = contract(turner, turned, 1, 0, near)
    turn = Exchange(turned.reshape(group, rank_dev, wide), [])
    turn.start_row()
    turn.got, basis_low = join(turn.got, basis_low)
    turn.finish()
    turns = turn.split(low, high)
    for turn in turns:
        turn.start()

    tile = cols // 7
    widths = [3 * tile, 4 * tile]

    def project(c):
        value = projection(starts, basis_low, grad, sizes, sum(widths[:c]), widths[c], tile)
        return Part(value.reshape((2,) * (dp_bits + row_bits) + (rank_dev, widths[c])), dp_bits, row_bits)

    front = project(0)
    front.value, basis_low, turns[0].got, turns[1].got = join(front.value, basis_low, turns[0].got, turns[1].got)
    front.start_row()
    for turn in turns:
        turn.finish()
        turn.start()
    back = project(1)
    back.value, front.got, turns[0].got, turns[1].got = join(back.value, front.got, turns[0].got, turns[1].got)
    front.finish()
    front = front.halves()
    for part, bit in zip(front, (low, high), strict=True):
        part.start("dp", bit)
    back.start_row()
    for turn in turns:
        turn.finish()
    (back.got,) = join(back.got)
    back.finish()
    back = back.halves()
    for part, bit in zip(back, (low, high), strict=True):
        part.start("dp", bit)
    front[0].got, front[1].got = join(front[0].got, front[1].got)
    for part, bit in zip(front, (high, low), strict=True):
        part.finish()
        part.start("dp", bit)
    back[0].got, back[1].got, front[0].got, front[1].got = join(back[0].got, back[1].got, front[0].got, front[1].got)
    for part, bit in zip(back, (high, low), strict=True):
        part.finish()
        part.start("dp", bit)
    for part in front:
        part.finish()
    back[0].got, back[1].got = join(back[0].got, back[1].got)
    for part in back:
        part.finish()
    projected = jnp.concatenate([part.value.reshape(rank_dev, -1) for part in front + back], 1)
    turned = jnp.concatenate([turn.result() for turn in turns], 1).reshape(2, group // 2, rank_dev, wide)
    turned = turned.transpose(0, 2, 1, 3).reshape(2, rank_dev, cols)
    first_new = 0.9 * turned[0] + 0.1 * projected
    second_new = 0.95 * turned[1] + 0.05 * projected * projected
    return (projected, first_new, second_new)


def solution(mesh):
    in_specs = (
        P("dp", "row", "col"),
        P("col", None),
        P("row", None),
        P(("dp", "row"), "col"),
        P(("dp", "row"), "col"),
    )
    out_specs = (P(("dp", "row"), "col"), P(("dp", "row"), "col"), P(("dp", "row"), "col"))
    return jax.shard_map(local, mesh=mesh, in_specs=in_specs, out_specs=out_specs, check_vma=False)
```
